256 devices in a mesh: row: 16 (over z_lo, x, core), col: 16 (over y, z_hi).
Axes of the slice: x: 4, y: 4, z: 8 (z_hi: 4, z_lo: 2; z = z_hi * 2 + z_lo), core: 2. Of those that a mesh axis runs over, the one named last changes fastest.
Arguments:
- gradient: bfloat16 [6144, 24576], P('row', 'col'), may hold values from -60 to 60
Outputs:
- update: bfloat16 [6144, 24576], P('row', 'col')
The draws below stay inside these ranges and needn't reach their ends.
All inputs are finite; a program needn't handle non-finite values.
Results may differ from the reference program's by a relative error of at most 0.001.
The reference program's roundings to bfloat16 on the way count: a program that leaves them out, or rounds other values in their place, can miss the bound.
Values may be sent and summed in bfloat16 or wider, within the bound.
No kernel may reach another device: no remote copies, remote signals or barrier semaphores. Data moves between devices by JAX's collectives and lax.ppermute only.
A program may use at most 128 MiB of HBM per device.

```python
import jax
import jax.numpy as jnp
from jax import lax

M = 6144
N = 24576
BLOCK = 1536


left_groups = 256


right_groups = 128


def draw_gradient(key, part):
    key = jax.random.fold_in(key, 7)
    keys = jax.random.split(key, 11)
    col_blocks = N // BLOCK
    rising = 3.0 ** (jnp.arange(M, dtype=jnp.float32) % BLOCK / BLOCK)
    column_group = jax.random.randint(keys[6], (N,), 0, left_groups)
    row_group = jax.random.randint(keys[7], (M,), 0, right_groups)
    values = jax.random.normal(keys[0], (M, N), jnp.float32)
    values = jnp.clip(values, -4.5, 4.5)
    row_scale = jnp.exp(jax.random.uniform(keys[1], (M, 1), jnp.float32, jnp.log(0.3), jnp.log(1.0)))
    mix_left = jnp.clip(jax.random.normal(keys[8], (M, left_groups), jnp.float32), -4.0, 4.0)
    mix_right = jnp.clip(jax.random.normal(keys[9], (right_groups, N), jnp.float32), -4.0, 4.0)
    row_scale = row_scale * rising[:, None]
    col_scale = jnp.exp(jax.random.uniform(keys[2], (1, N), jnp.float32, jnp.log(0.3), jnp.log(3.0)))
    left_vectors = jnp.clip(jax.random.normal(keys[4], (M, col_blocks), jnp.float32), -3.0, 3.0)
    right_vector = jnp.clip(jax.random.normal(keys[5], (1, N), jnp.float32), -3.0, 3.0)
    amplitude = 0.6 * 2.7 ** (jnp.arange(col_blocks, dtype=jnp.float32) / max(col_blocks - 1, 1))
    spread_left = jnp.repeat(left_vectors * amplitude[None, :], BLOCK, axis=1)
    spike = spread_left * right_vector
    col_weight = jnp.exp(jax.random.uniform(keys[10], (1, N), jnp.float32, jnp.log(0.5), jnp.log(2.0)))
    dense_left = jnp.take(mix_left, column_group, axis=1) * col_weight
    dense_right = jnp.take(mix_right, row_group, axis=0)
    mixed = values * row_scale * col_scale + spike + row_scale * (1.2 * dense_left + 0.8 * dense_right)
    return jnp.clip(mixed, -59.0, 59.0).astype(jnp.bfloat16)


def setup_inputs(seed: int = 0) -> dict:
    key_list = jax.random.split(jax.random.key(seed), 2)
    return {
        "gradient": draw_gradient(jax.random.fold_in(key_list[1], 71), 0),
    }


damping = 0.001

def root_of(gram):
    scale_value = jnp.sqrt(jnp.sum(gram * gram))
    identity = jnp.eye(BLOCK, dtype=jnp.float32)
    return ((5.0 * identity - gram / scale_value) * 0.25 * scale_value ** (-0.25)).astype(jnp.bfloat16)

def reference(gradient):
    rows_blocks = M // BLOCK
    cols_blocks = N // BLOCK
    identity = jnp.eye(BLOCK, dtype=jnp.float32)
    bands = gradient.reshape(rows_blocks, BLOCK, N)

    def left_block(band):
        gram = lax.dot_general(band, band, (((1,), (1,)), ((), ())), preferred_element_type=jnp.float32)
        return root_of(gram + damping * identity)
    left_roots = lax.map(left_block, bands)
    left_wide = left_roots.astype(jnp.float32)
    stripes = jnp.transpose(gradient.reshape(M, cols_blocks, BLOCK), (1, 0, 2))

    def column_block(stripe):
        gram = lax.dot_general(stripe, stripe, (((0,), (0,)), ((), ())), preferred_element_type=jnp.float32)
        right_root = root_of(gram + damping * identity)
        projected = jnp.dot(stripe, right_root, preferred_element_type=jnp.float32).astype(jnp.bfloat16)
        tiles = projected.reshape(rows_blocks, BLOCK, BLOCK).astype(jnp.float32)
        precond = jnp.einsum('ikl,ild->ikd', left_wide, tiles, precision=lax.Precision.HIGHEST)
        grad_tiles = stripe.reshape(rows_blocks, BLOCK, BLOCK).astype(jnp.float32)
        grad_sq = lax.optimization_barrier(jnp.sum(grad_tiles * grad_tiles, axis=(1, 2)))
        pre_sq = lax.optimization_barrier(jnp.sum(precond * precond, axis=(1, 2)))
        factor = jnp.sqrt(grad_sq) / jnp.sqrt(pre_sq + 1e-06)
        return (precond * factor[:, None, None]).astype(jnp.bfloat16)
    result = lax.map(column_block, stripes)
    return jnp.transpose(result, (1, 2, 0, 3)).reshape(M, N)
```

```python
import functools

import jax
import jax.numpy as jnp
from jax import lax
from jax.experimental import pallas as pl
from jax.experimental.pallas import tpu as pltpu
from jax.sharding import PartitionSpec as P

BLOCK = 1536
ROWS = 384
LANE = 128
BLOCKS = BLOCK // LANE
BAND = 7
HALF = BLOCK // 2
RIGHT = 192
LEFT = 192
PIECE = 48
RIGHT_CUTS = ((0, 4), (4, 7))

damping = 0.001
F32 = jnp.float32
BF16 = jnp.bfloat16
MIB = 1 << 20

SMEM = pl.BlockSpec(memory_space=pltpu.SMEM)
VMEM = pl.BlockSpec(memory_space=pltpu.VMEM)
ANY = pl.BlockSpec(memory_space=pl.ANY)


def params(mib):
    return pltpu.CompilerParams(vmem_limit_bytes=mib * MIB)


def sds(shape, dtype):
    return jax.ShapeDtypeStruct(shape, dtype)


def hop(value, axis, mask):
    return lax.ppermute(value, axis, [(i, i ^ mask) for i in range(16)])


def folded(wide):
    rows, cols = wide.shape
    tall = jnp.sum(wide.reshape(rows // 8, 8, cols), axis=0)
    total = tall[:, :LANE]
    for start in range(LANE, cols, LANE):
        total = total + tall[:, start : start + LANE]
    return total


def squares(ref):
    total = jnp.zeros((8, LANE), F32)
    for start in range(0, ref.shape[0], 48):
        part = ref[start : start + 48, :].astype(F32)
        total = total + folded(part * part)
    return total


def nt(a, b):
    return lax.dot_general(a, b, (((1,), (1,)), ((), ())), preferred_element_type=F32)


def grams_kernel(place, mine, other, *refs):
    right_outs = refs[: 4 * len(RIGHT_CUTS)]
    left_outs = refs[4 * len(RIGHT_CUTS) : 4 * len(RIGHT_CUTS) + 4]
    square_out, wide, right_all, left_all, sems = refs[4 * len(RIGHT_CUTS) + 4 :]
    core, block, row_y = place[0], place[1], place[2]
    copies = []
    for at, source in enumerate((mine, other)):
        rows = pl.ds(at * ROWS, ROWS)
        copies.append(pltpu.make_async_copy(source, wide.at[rows, pl.ds(0, BLOCK)], sems.at[2 * at]))
        copies.append(
            pltpu.make_async_copy(
                source.at[:, pl.ds(0, HALF)], wide.at[rows, pl.ds(BLOCK, HALF)], sems.at[2 * at + 1]
            )
        )
    for copy in copies:
        copy.start()
    for copy in copies:
        copy.wait()
    for pair in range(3):
        start = pl.multiple_of(core * HALF + pair * 256, LANE)
        strip = wide[:, pl.ds(start, 1024)]
        gram = lax.dot_general(
            strip[:, :256], strip, (((0,), (0,)), ((), ())), preferred_element_type=F32
        ).astype(BF16)
        for half in range(2):
            at = pair * 256 + half * LANE
            right_all[at : at + LANE, :] = gram[
                half * LANE : half * LANE + LANE, half * LANE : half * LANE + BAND * LANE
            ]
    for slot in range(4):
        start = pl.multiple_of((block ^ slot) * RIGHT, 16)
        for cut, (low, high) in enumerate(RIGHT_CUTS):
            right_outs[4 * cut + slot][...] = right_all[
                pl.ds(start, RIGHT), low * LANE : high * LANE
            ]
    for at in range(2):
        left_all[at * ROWS : (at + 1) * ROWS, :] = nt(
            wide[:ROWS, :BLOCK], wide[at * ROWS : (at + 1) * ROWS, :BLOCK]
        ).astype(BF16)
    for slot in range(4):
        start = pl.multiple_of((row_y ^ slot) * LEFT, 16)
        left_outs[slot][...] = left_all[pl.ds(start, LEFT), :]
    square_out[...] = squares(wide.at[:, pl.ds(0, BLOCK)])


def grams(place, mine, other):
    shapes = [
        sds((RIGHT, (high - low) * LANE), BF16) for low, high in RIGHT_CUTS for _ in range(4)
    ]
    shapes += [sds((LEFT, ROWS), BF16)] * 4 + [sds((8, LANE), F32)]
    return pl.pallas_call(
        grams_kernel,
        out_shape=shapes,
        in_specs=[SMEM, ANY, ANY],
        out_specs=[VMEM] * len(shapes),
        scratch_shapes=[
            pltpu.VMEM((2 * ROWS, BLOCK + HALF), BF16),
            pltpu.VMEM((HALF, BAND * LANE), BF16),
            pltpu.VMEM((2 * ROWS, ROWS), BF16),
            pltpu.SemaphoreType.DMA((4,)),
        ],
        compiler_params=params(40),
        cost_estimate=pl.CostEstimate(flops=3 * 10**9, bytes_accessed=6 * 10**6, transcendentals=0),
        name="grams",
    )(place, mine, other)


def cross_kernel(place, mine, first, second, *refs):
    left_outs = refs[:4]
    square_out, left_all = refs[4:]
    row_y = place[2]
    for at, source in enumerate((first, second)):
        left_all[at * ROWS : (at + 1) * ROWS, :] = nt(mine[...], source[...]).astype(BF16)
    for slot in range(4):
        start = pl.multiple_of((row_y ^ slot) * LEFT, 16)
        left_outs[slot][...] = left_all[pl.ds(start, LEFT), :]
    square_out[...] = squares(first) + squares(second)


def cross(place, mine, first, second):
    shapes = [sds((LEFT, ROWS), BF16)] * 4 + [sds((8, LANE), F32)]
    return pl.pallas_call(
        cross_kernel,
        out_shape=shapes,
        in_specs=[SMEM, VMEM, VMEM, VMEM],
        out_specs=[VMEM] * len(shapes),
        scratch_shapes=[pltpu.VMEM((2 * ROWS, ROWS), BF16)],
        compiler_params=params(40),
        cost_estimate=pl.CostEstimate(flops=10**9, bytes_accessed=4 * 10**6, transcendentals=0),
        name="cross",
    )(place, mine, first, second)


def split_kernel(place, a, b, c, d, *refs):
    outs, total = refs[:4], refs[4]
    total[...] = (a[...].astype(F32) + b[...].astype(F32)) + (c[...].astype(F32) + d[...].astype(F32))
    for slot in range(4):
        start = pl.multiple_of((place[3] ^ slot) * PIECE, 16)
        outs[slot][...] = total[pl.ds(start, PIECE), :].astype(BF16)


def split(place, parts):
    return pl.pallas_call(
        split_kernel,
        out_shape=[sds((PIECE, ROWS), BF16)] * 4,
        in_specs=[SMEM] + [VMEM] * 4,
        out_specs=[VMEM] * 4,
        scratch_shapes=[pltpu.VMEM((LEFT, ROWS), F32)],
        compiler_params=params(16),
        cost_estimate=pl.CostEstimate(flops=10**6, bytes_accessed=10**6, transcendentals=0),
        name="split",
    )(place, *parts)


def left_rows_kernel(place, *refs):
    parts, (rows_out, square_out) = refs[:8], refs[8:]
    row_y, col_z = place[2], place[3]
    for at in range(8):
        shard = (row_y ^ (at % 4)) + 4 * (at // 4)
        lanes = pl.ds(pl.multiple_of(shard // 2 * ROWS, LANE), ROWS)
        for slot in range(4):
            start = pl.multiple_of(shard % 2 * LEFT + (col_z ^ slot) * PIECE, 16)
            rows_out[pl.ds(start, PIECE), lanes] = parts[at][slot * PIECE : (slot + 1) * PIECE, :]
    own = rows_out[:, :ROWS].astype(F32)
    shape = (ROWS, ROWS)
    eye = lax.broadcasted_iota(jnp.int32, shape, 0) == lax.broadcasted_iota(jnp.int32, shape, 1)
    own = own + jnp.where(eye, damping, 0.0)
    square_out[...] = folded(own * own) + squares(rows_out.at[:, pl.ds(ROWS, BLOCK - ROWS)])


def left_rows(place, parts):
    return pl.pallas_call(
        left_rows_kernel,
        out_shape=[sds((ROWS, BLOCK), BF16), sds((8, LANE), F32)],
        in_specs=[SMEM] + [VMEM] * 8,
        out_specs=[VMEM] * 2,
        compiler_params=params(24),
        cost_estimate=pl.CostEstimate(flops=10**6, bytes_accessed=2 * 10**6, transcendentals=0),
        name="left_rows",
    )(place, *parts)


def scale_of(total):
    total = jnp.sum(total, axis=1, keepdims=True)
    total = jnp.sum(total, axis=0, keepdims=True)
    return jnp.sqrt(jnp.broadcast_to(total, (1, LANE)))


def widened(row, width):
    return jnp.concatenate([row] * (width // LANE), axis=1)


def projected_kernel(place, *refs):
    count = 8 * len(RIGHT_CUTS)
    parts, tiles = refs[:count], refs[count : count + 4]
    out, packed, root, band, sems, band_sems = refs[count + 4 :]
    core, block = place[0], place[1]
    copies = []
    for cut, (low, high) in enumerate(RIGHT_CUTS):
        for side in range(2):
            for slot in range(4):
                at = cut * 8 + side * 4 + slot
                start = pl.multiple_of((core ^ side) * HALF + (block ^ slot) * RIGHT, 16)
                copies.append(
                    pltpu.make_async_copy(
                        parts[at],
                        packed.at[pl.ds(start, RIGHT), pl.ds(low * LANE, (high - low) * LANE)],
                        sems.at[at],
                    )
                )
    band_copies = [
        pltpu.make_async_copy(tiles[at], band.at[pl.ds(at * ROWS, ROWS), :], band_sems.at[at])
        for at in range(4)
    ]
    for copy in copies + band_copies:
        copy.start()
    for copy in copies:
        copy.wait()
    shape = (LANE, LANE)
    eye = lax.broadcasted_iota(jnp.int32, shape, 0) == lax.broadcasted_iota(jnp.int32, shape, 1)
    total = jnp.zeros((8, LANE), F32)
    for row in range(BLOCKS):
        strip = packed[row * LANE : (row + 1) * LANE, :].astype(F32)
        head = strip[:, :LANE] + jnp.where(eye, damping, 0.0)
        tail = strip[:, 6 * LANE :]
        middle = strip[:, LANE : 6 * LANE]
        total = total + folded(head * head) + folded(tail * tail) + 2.0 * folded(middle * middle)
    scale = scale_of(total)
    factor = 0.25 / jnp.sqrt(jnp.sqrt(scale))
    inverse = 1.0 / scale
    for row in range(BLOCKS):
        for apart in range(BAND):
            part = packed[row * LANE : (row + 1) * LANE, apart * LANE : (apart + 1) * LANE]
            part = part.astype(F32)
            if apart == 0:
                part = jnp.where(eye, 5.0 - (part + damping) * inverse, -part * inverse)
                part = part * factor
            else:
                part = (-part * inverse) * factor
            col = (row + apart) % BLOCKS
            root[row * LANE : (row + 1) * LANE, col * LANE : (col + 1) * LANE] = part.astype(BF16)
            if 0 < apart < 6:
                root[col * LANE : (col + 1) * LANE, row * LANE : (row + 1) * LANE] = part.T.astype(BF16)
    for copy in band_copies:
        copy.wait()

    def step(at, carry):
        rows = pl.ds(pl.multiple_of(at * ROWS, 16), ROWS)
        for start in range(0, BLOCK, 512):
            out[rows, start : start + 512] = jnp.dot(
                band[rows, :], root[:, start : start + 512], preferred_element_type=F32
            ).astype(BF16)
        return carry

    lax.fori_loop(0, 4, step, 0)


def projected_band(place, parts, tiles):
    return pl.pallas_call(
        projected_kernel,
        out_shape=sds((BLOCK, BLOCK), BF16),
        in_specs=[SMEM] + [ANY] * (len(parts) + 4),
        out_specs=VMEM,
        scratch_shapes=[
            pltpu.VMEM((BLOCK, BAND * LANE), BF16),
            pltpu.VMEM((BLOCK, BLOCK), BF16),
            pltpu.VMEM((BLOCK, BLOCK), BF16),
            pltpu.SemaphoreType.DMA((len(parts),)),
            pltpu.SemaphoreType.DMA((4,)),
        ],
        compiler_params=params(48),
        cost_estimate=pl.CostEstimate(flops=72 * 10**8, bytes_accessed=12 * 10**6, transcendentals=0),
        name="projected",
    )(place, *parts, *tiles)


def precond_kernel(a, b, c, d, rows, projected, out, square_out, root):
    scale = scale_of((a[...] + b[...]) + (c[...] + d[...]))
    factor = 0.25 / jnp.sqrt(jnp.sqrt(scale))
    inverse = 1.0 / scale
    shape = (ROWS, ROWS)
    eye = lax.broadcasted_iota(jnp.int32, shape, 0) == lax.broadcasted_iota(jnp.int32, shape, 1)
    inverse, factor = widened(inverse, ROWS), widened(factor, ROWS)
    own = rows[:, :ROWS].astype(F32)
    own = jnp.where(eye, 5.0 - (own + damping) * inverse, -own * inverse) * factor
    root[:, :ROWS] = own.astype(BF16)
    for start in range(ROWS, BLOCK, ROWS):
        part = rows[:, start : start + ROWS].astype(F32)
        root[:, start : start + ROWS] = ((-part * inverse) * factor).astype(BF16)
    total = jnp.zeros((8, LANE), F32)
    for start in range(0, BLOCK, 256):
        part = jnp.dot(root[...], projected[:, start : start + 256], preferred_element_type=F32)
        out[:, start : start + 256] = part
        total = total + folded(part * part)
    square_out[...] = total


def precond(totals, rows, projected):
    return pl.pallas_call(
        precond_kernel,
        out_shape=[sds((ROWS, BLOCK), F32), sds((8, LANE), F32)],
        in_specs=[VMEM] * 6,
        out_specs=[VMEM] * 2,
        scratch_shapes=[pltpu.VMEM((ROWS, BLOCK), BF16)],
        compiler_params=params(40),
        cost_estimate=pl.CostEstimate(flops=18 * 10**8, bytes_accessed=8 * 10**6, transcendentals=0),
        name="precond",
    )(*totals, rows, projected)


def graft_kernel(grad_a, grad_b, a, b, c, d, value, out):
    grad = scale_of(grad_a[...] + grad_b[...])
    pre = (a[...] + b[...]) + (c[...] + d[...])
    pre = jnp.sum(jnp.sum(pre, axis=1, keepdims=True), axis=0, keepdims=True)
    factor = grad / jnp.sqrt(jnp.broadcast_to(pre, (1, LANE)) + 1e-06)
    out[...] = (value[...] * widened(factor, BLOCK)).astype(BF16)


def graft(grad_parts, totals, value):
    step = 96
    small = pl.BlockSpec((8, LANE), lambda i: (0, 0))
    wide = pl.BlockSpec((step, BLOCK), lambda i: (i, 0))
    return pl.pallas_call(
        graft_kernel,
        grid=(ROWS // step,),
        out_shape=sds((ROWS, BLOCK), BF16),
        in_specs=[small] * 6 + [wide],
        out_specs=wide,
        compiler_params=params(24),
        cost_estimate=pl.CostEstimate(flops=10**6, bytes_accessed=4 * 10**6, transcendentals=0),
        name="graft",
    )(*grad_parts, *totals, value)


def total_of(parts):
    total = parts[0].astype(F32)
    for part in parts[1:]:
        total = total + part.astype(F32)
    return total.astype(BF16)


def exchanged(parts, axis, masks):
    return [parts[0]] + [hop(part, axis, mask) for part, mask in zip(parts[1:], masks)]


def spread(value, axis, masks):
    return [value] + [hop(value, axis, mask) for mask in masks]


CORE, NEAR, FAR, ACROSS = 1, 2, 6, 8
RING = (ACROSS, FAR, ACROSS | FAR)
UP = (4, 8, 12)
DEEP = (1, 2, 3)


def left_shards(place, slots):
    slots = exchanged(slots, "col", UP)
    pieces = exchanged(split(place, slots), "col", DEEP)
    pieces = spread(total_of(pieces), "col", DEEP)
    return spread(jnp.concatenate(pieces, axis=0), "col", UP)


def local(gradient):
    row, col = lax.axis_index("row"), lax.axis_index("col")
    core, x, z_low = row % 2, row // 2 % 4, row // 8
    place = jnp.stack([core, x // 2 * 2 + z_low, col // 4, col % 4]).astype(jnp.int32)
    other = hop(gradient, "row", CORE)
    near = hop(gradient, "row", NEAR)
    near_other = hop(near, "row", CORE)
    *outs, grad_a = grams(place, gradient, other)
    parts = []
    for cut in range(len(RIGHT_CUTS)):
        slots = exchanged(outs[4 * cut : 4 * cut + 4], "row", RING)
        mine = total_of(slots)
        mine = total_of([mine, hop(mine, "row", NEAR)])
        slots = spread(mine, "row", RING)
        parts += slots + [hop(slot, "row", CORE) for slot in slots]
    diagonal = left_shards(place, outs[-4:])
    *outs, grad_b = cross(place, gradient, near, near_other)
    offside = left_shards(place, outs)
    rows, square = left_rows(place, diagonal + offside)
    totals = spread(square, "row", (CORE, NEAR, CORE | NEAR))
    projected = projected_band(place, parts, (gradient, other, near, near_other))
    value, square = precond(totals, rows, projected)
    totals = spread(square, "row", (CORE, NEAR, CORE | NEAR))
    return graft((grad_a, grad_b), totals, value)


def solution(mesh):
    return jax.shard_map(
        local, mesh=mesh, in_specs=(P("row", "col"),), out_specs=P("row", "col"), check_vma=False
    )
```

```python
import jax
import jax.numpy as jnp
from jax import lax
from jax.experimental import pallas as pl
from jax.experimental.pallas import tpu as pltpu
from jax.sharding import PartitionSpec as P

BLOCK = 1536
ROWS = 384
LANE = 128
BLOCKS = BLOCK // LANE
BAND = 7
HALF = BLOCK // 2
RIGHT = 192
LEFT = 96

damping = 0.001
F32 = jnp.float32
BF16 = jnp.bfloat16
MIB = 1 << 20

SMEM = pl.BlockSpec(memory_space=pltpu.SMEM)
VMEM = pl.BlockSpec(memory_space=pltpu.VMEM)
ANY = pl.BlockSpec(memory_space=pl.ANY)


def params(mib):
    return pltpu.CompilerParams(vmem_limit_bytes=mib * MIB)


def cost(flops, moved):
    return pl.CostEstimate(flops=flops, bytes_accessed=moved, transcendentals=0)


def sds(shape, dtype):
    return jax.ShapeDtypeStruct(shape, dtype)


def hop(value, axis, mask):
    return lax.ppermute(value, axis, [(i, i ^ mask) for i in range(16)])


def folded(wide):
    rows, cols = wide.shape
    tall = jnp.sum(wide.reshape(rows // 8, 8, cols), axis=0)
    total = tall[:, :LANE]
    for start in range(LANE, cols, LANE):
        total = total + tall[:, start : start + LANE]
    return total


def squares(ref):
    total = jnp.zeros((8, LANE), F32)
    for start in range(0, ref.shape[0], 48):
        part = ref[start : start + 48, :].astype(F32)
        total = total + folded(part * part)
    return total


def nt(a, b):
    return lax.dot_general(a, b, (((1,), (1,)), ((), ())), preferred_element_type=F32)


def dealt(whole, outs, rows, place, first):
    for slot in range(4):
        start = pl.multiple_of(place[first + slot] * rows, 16)
        at = slot % 2 * rows
        outs[slot // 2][at : at + rows, :] = whole[pl.ds(start, rows), :]


def right_kernel(place, mine, other, keep, send, wide, whole, sems):
    copies = []
    for at, source in enumerate((mine, other)):
        rows = pl.ds(at * ROWS, ROWS)
        copies.append(pltpu.make_async_copy(source, wide.at[rows, pl.ds(0, BLOCK)], sems.at[2 * at]))
        copies.append(
            pltpu.make_async_copy(
                source.at[:, pl.ds(0, HALF)], wide.at[rows, pl.ds(BLOCK, HALF)], sems.at[2 * at + 1]
            )
        )
    for copy in copies:
        copy.start()
    for copy in copies:
        copy.wait()
    for pair in range(3):
        start = pl.multiple_of(place[0] * HALF + pair * 256, LANE)
        strip = wide[:, pl.ds(start, 1024)]
        gram = lax.dot_general(
            strip[:, :256], strip, (((0,), (0,)), ((), ())), preferred_element_type=F32
        ).astype(BF16)
        for half in range(2):
            at = pair * 256 + half * LANE
            whole[at : at + LANE, :] = gram[
                half * LANE : half * LANE + LANE, half * LANE : half * LANE + BAND * LANE
            ]
    dealt(whole, (keep, send), RIGHT, place, 1)


def right_gram(place, mine, other):
    return pl.pallas_call(
        right_kernel,
        out_shape=[sds((2 * RIGHT, BAND * LANE), BF16)] * 2,
        in_specs=[SMEM, ANY, ANY],
        out_specs=[VMEM] * 2,
        scratch_shapes=[
            pltpu.VMEM((2 * ROWS, BLOCK + HALF), BF16),
            pltpu.VMEM((HALF, BAND * LANE), BF16),
            pltpu.SemaphoreType.DMA((4,)),
        ],
        compiler_params=params(32),
        cost_estimate=cost(10**6, 10**4),
        name="right_gram",
    )(place, mine, other)


def own_kernel(place, mine, other, keep, send, square_out, whole):
    for at, source in enumerate((mine, other)):
        whole[:, at * ROWS : (at + 1) * ROWS] = nt(mine[...], source[...]).astype(BF16)
    dealt(whole, (keep, send), LEFT, place, 5)
    square_out[...] = squares(mine)


def own_gram(place, mine, other):
    half = sds((2 * LEFT, 2 * ROWS), BF16)
    return pl.pallas_call(
        own_kernel,
        out_shape=[half, half, sds((8, LANE), F32)],
        in_specs=[SMEM, VMEM, VMEM],
        out_specs=[VMEM] * 3,
        scratch_shapes=[pltpu.VMEM((ROWS, 2 * ROWS), BF16)],
        compiler_params=params(24),
        cost_estimate=cost(10**6, 10**4),
        name="own_gram",
    )(place, mine, other)


def cross_kernel(place, mine, other, near, keep, send, whole):
    upper = place[9]
    half = pl.ds(pl.multiple_of(upper * HALF, LANE), HALF)
    for at, source in enumerate((mine, other)):
        span = slice(at * ROWS, (at + 1) * ROWS)

        @pl.when(upper == 0)
        def _():
            whole[:, span] = nt(source[:, half], near[...]).astype(BF16)

        @pl.when(upper == 1)
        def _():
            whole[:, span] = nt(near[...], source[:, half]).astype(BF16)

    dealt(whole, (keep, send), LEFT, place, 5)


def cross_gram(place, mine, other, near):
    return pl.pallas_call(
        cross_kernel,
        out_shape=[sds((2 * LEFT, 2 * ROWS), BF16)] * 2,
        in_specs=[SMEM] + [VMEM] * 3,
        out_specs=[VMEM] * 2,
        scratch_shapes=[pltpu.VMEM((ROWS, 2 * ROWS), BF16)],
        compiler_params=params(24),
        cost_estimate=cost(10**6, 10**4),
        name="cross_gram",
    )(place, mine, other, near)


def left_rows_kernel(place, low, high, rows_out, square_out, cross):
    for slot in range(4):
        rows = pl.ds(pl.multiple_of(place[5 + slot] * LEFT, 16), LEFT)
        span = slice(slot % 2 * LEFT, slot % 2 * LEFT + LEFT)
        rows_out[rows, : 2 * ROWS] = (low, high)[slot // 2][span, : 2 * ROWS]
        cross[rows, :] = (low, high)[slot // 2][span, 2 * ROWS :]

    @pl.when(place[9] == 0)
    def _():
        rows_out[:, 2 * ROWS :] = cross[...]

    @pl.when(place[9] == 1)
    def _():
        for at in range(2):
            part = cross[:, at * ROWS : (at + 1) * ROWS].astype(F32).T
            rows_out[:, (2 + at) * ROWS : (3 + at) * ROWS] = part.astype(BF16)

    own = rows_out[:, :ROWS].astype(F32)
    shape = (ROWS, ROWS)
    eye = lax.broadcasted_iota(jnp.int32, shape, 0) == lax.broadcasted_iota(jnp.int32, shape, 1)
    own = own + jnp.where(eye, damping, 0.0)
    square_out[...] = folded(own * own) + squares(rows_out.at[:, pl.ds(ROWS, BLOCK - ROWS)])


def left_rows(place, parts):
    return pl.pallas_call(
        left_rows_kernel,
        out_shape=[sds((ROWS, BLOCK), BF16), sds((8, LANE), F32)],
        in_specs=[SMEM] + [VMEM] * 2,
        out_specs=[VMEM] * 2,
        scratch_shapes=[pltpu.VMEM((ROWS, 2 * ROWS), BF16)],
        compiler_params=params(24),
        cost_estimate=cost(10**6, 2 * 10**6),
        name="left_rows",
    )(place, *parts)


def scale_of(total):
    total = jnp.sum(total, axis=1, keepdims=True)
    total = jnp.sum(total, axis=0, keepdims=True)
    return jnp.sqrt(jnp.broadcast_to(total, (1, LANE)))


def widened(row, width):
    return jnp.concatenate([row] * (width // LANE), axis=1)


def root_kernel(place, *refs):
    parts, (root, packed, sems) = refs[:4], refs[4:]
    core = place[0]
    copies = []
    for side in range(2):
        for slot in range(4):
            turned = slot if side == 0 or slot in (0, 3) else 3 - slot
            start = pl.multiple_of((core ^ side) * HALF + place[1 + turned] * RIGHT, 16)
            copies.append(
                pltpu.make_async_copy(
                    parts[2 * side + slot // 2].at[pl.ds(slot % 2 * RIGHT, RIGHT), :],
                    packed.at[pl.ds(start, RIGHT), :],
                    sems.at[4 * side + slot],
                )
            )
    for copy in copies:
        copy.start()
    for copy in copies:
        copy.wait()
    shape = (LANE, LANE)
    eye = lax.broadcasted_iota(jnp.int32, shape, 0) == lax.broadcasted_iota(jnp.int32, shape, 1)
    total = jnp.zeros((8, LANE), F32)
    for row in range(BLOCKS):
        strip = packed[row * LANE : (row + 1) * LANE, :].astype(F32)
        head = strip[:, :LANE] + jnp.where(eye, damping, 0.0)
        tail = strip[:, 6 * LANE :]
        middle = strip[:, LANE : 6 * LANE]
        total = total + folded(head * head) + folded(tail * tail) + 2.0 * folded(middle * middle)
    scale = scale_of(total)
    factor = 0.25 / jnp.sqrt(jnp.sqrt(scale))
    inverse = 1.0 / scale
    for row in range(BLOCKS):
        for apart in range(BAND):
            part = packed[row * LANE : (row + 1) * LANE, apart * LANE : (apart + 1) * LANE]
            part = part.astype(F32)
            if apart == 0:
                part = jnp.where(eye, 5.0 - (part + damping) * inverse, -part * inverse)
                part = part * factor
            else:
                part = (-part * inverse) * factor
            col = (row + apart) % BLOCKS
            root[row * LANE : (row + 1) * LANE, col * LANE : (col + 1) * LANE] = part.astype(BF16)
            if 0 < apart < 6:
                root[col * LANE : (col + 1) * LANE, row * LANE : (row + 1) * LANE] = part.T.astype(BF16)


def right_root(place, parts):
    return pl.pallas_call(
        root_kernel,
        out_shape=sds((BLOCK, BLOCK), BF16),
        in_specs=[SMEM] + [ANY] * 4,
        out_specs=VMEM,
        scratch_shapes=[pltpu.VMEM((BLOCK, BAND * LANE), BF16), pltpu.SemaphoreType.DMA((8,))],
        compiler_params=params(24),
        cost_estimate=cost(10**7, 8 * 10**6),
        name="right_root",
    )(place, *parts)


def product_kernel(tile, root, out):
    for start in range(0, BLOCK, 512):
        out[:, start : start + 512] = jnp.dot(
            tile[...], root[:, start : start + 512], preferred_element_type=F32
        ).astype(BF16)


def near_product_kernel(place, first, second, root, out):
    upper = place[9]
    top = pl.ds(pl.multiple_of(upper * HALF, 16), HALF)
    rest = pl.ds(pl.multiple_of((1 - upper) * HALF, 16), HALF)
    for start in range(0, BLOCK, 512):
        span = slice(start, start + 512)
        part = jnp.dot(first[...], root[top, span], preferred_element_type=F32)
        part = part + jnp.dot(second[...], root[rest, span], preferred_element_type=F32)
        out[:, span] = part.astype(BF16)


def product(root, tile, *more):
    near = [tile, *more]
    return pl.pallas_call(
        near_product_kernel if more else product_kernel,
        out_shape=sds((ROWS, BLOCK), BF16),
        in_specs=([SMEM] if more else []) + [VMEM] * (len(near) - 1 if more else len(near)) + [VMEM],
        out_specs=VMEM,
        compiler_params=params(24),
        cost_estimate=cost(18 * 10**8, 7 * 10**6),
        name="product",
    )(*near, root)


def precond_kernel(a, b, c, d, rows, p0, p1, p2, p3, grad, out, square_out, root):
    scale = scale_of((a[...] + b[...]) + (c[...] + d[...]))
    factor = 0.25 / jnp.sqrt(jnp.sqrt(scale))
    inverse = 1.0 / scale
    shape = (ROWS, ROWS)
    eye = lax.broadcasted_iota(jnp.int32, shape, 0) == lax.broadcasted_iota(jnp.int32, shape, 1)
    inverse, factor = widened(inverse, ROWS), widened(factor, ROWS)
    own = rows[:, :ROWS].astype(F32)
    own = jnp.where(eye, 5.0 - (own + damping) * inverse, -own * inverse) * factor
    root[:, :ROWS] = own.astype(BF16)
    for start in range(ROWS, BLOCK, ROWS):
        part = rows[:, start : start + ROWS].astype(F32)
        root[:, start : start + ROWS] = ((-part * inverse) * factor).astype(BF16)
    total = jnp.zeros((8, LANE), F32)
    for start in range(0, BLOCK, 256):
        part = jnp.dot(root[:, :ROWS], p0[:, start : start + 256], preferred_element_type=F32)
        for at, tile in ((1, p1), (2, p2), (3, p3)):
            part = part + jnp.dot(
                root[:, at * ROWS : (at + 1) * ROWS],
                tile[:, start : start + 256],
                preferred_element_type=F32,
            )
        out[:, start : start + 256] = part
        total = total + folded(part * part)
    square_out[:8, :] = total
    square_out[8:, :] = grad[...]


def precond(totals, rows, tiles, grad):
    return pl.pallas_call(
        precond_kernel,
        out_shape=[sds((ROWS, BLOCK), F32), sds((16, LANE), F32)],
        in_specs=[VMEM] * 10,
        out_specs=[VMEM] * 2,
        scratch_shapes=[pltpu.VMEM((ROWS, BLOCK), BF16)],
        compiler_params=params(40),
        cost_estimate=cost(18 * 10**8, 8 * 10**6),
        name="precond",
    )(*totals, rows, *tiles, grad)


def graft_kernel(a, b, c, d, value, out):
    total = (a[...] + b[...]) + (c[...] + d[...])
    pre = jnp.sum(jnp.sum(total[:8, :], axis=1, keepdims=True), axis=0, keepdims=True)
    factor = scale_of(total[8:, :]) / jnp.sqrt(jnp.broadcast_to(pre, (1, LANE)) + 1e-06)
    out[...] = (value[...] * widened(factor, BLOCK)).astype(BF16)


def graft(totals, value):
    step = 96
    small = pl.BlockSpec((16, LANE), lambda i: (0, 0))
    wide = pl.BlockSpec((step, BLOCK), lambda i: (i, 0))
    return pl.pallas_call(
        graft_kernel,
        grid=(ROWS // step,),
        out_shape=sds((ROWS, BLOCK), BF16),
        in_specs=[small] * 4 + [wide],
        out_specs=wide,
        compiler_params=params(24),
        cost_estimate=cost(10**6, 4 * 10**6),
        name="graft",
    )(*totals, value)


def total_of(a, b):
    return a.astype(F32) + b.astype(F32)


CORE, NEAR, FAR, ACROSS = 1, 2, 6, 8
ROUND = ((FAR, ACROSS), (ACROSS, FAR))
UP = ((4, 12), (12, 4))
DEEP = ((1, 3), (3, 1))


def turned(value, masks, at):
    pairs = []
    for device in range(256):
        mask = masks[device // 16 % 2][at]
        mask = mask * 16 if masks is ROUND else mask
        pairs.append((device, device ^ mask))
    return lax.ppermute(value, ("row", "col"), pairs)


def after(value, *tokens):
    return lax.optimization_barrier((value, tokens))[0]


def spread(value):
    return [value] + [hop(value, "row", mask) for mask in (CORE, NEAR, CORE | NEAR)]


def right_steps(keep, send):
    tokens = yield
    came = turned(after(send, *tokens), ROUND, 0)
    total = total_of(keep, came)
    tokens = yield came
    came = turned(after(total[RIGHT:].astype(BF16), *tokens), ROUND, 1)
    mine = total_of(total[:RIGHT], came).astype(BF16)
    tokens = yield came
    came = hop(after(mine, *tokens), "row", NEAR)
    mine = total_of(mine, came).astype(BF16)
    tokens = yield came
    came = turned(after(mine, *tokens), ROUND, 1)
    low = jnp.concatenate([mine, came], axis=0)
    tokens = yield came
    low = after(low, *tokens)
    high = turned(low, ROUND, 0)
    low_other = hop(low, "row", CORE)
    tokens = yield high
    high_other = hop(after(high, *tokens), "row", CORE)
    yield high_other
    yield [low, high, low_other, high_other]


def scatter_steps(keep, send):
    tokens = yield
    came = turned(after(send, *tokens), UP, 0)
    total = total_of(keep, came)
    tokens = yield came
    came = turned(after(total[LEFT:].astype(BF16), *tokens), UP, 1)
    yield came
    yield total_of(total[:LEFT], came).astype(BF16)


def deep_steps(mine):
    for at in range(2):
        tokens = yield
        came = turned(after(mine, *tokens), DEEP, at)
        mine = total_of(mine, came).astype(BF16)
        yield came
    yield mine


def pair_step(mine, tokens):
    mine = after(mine, *tokens)
    near = hop(mine, "row", NEAR)
    core = hop(mine[:, ROWS:], "row", CORE)
    first = total_of(mine[:, :ROWS], near[:, :ROWS]).astype(BF16)
    second = total_of(core, near[:, ROWS:]).astype(BF16)
    return near, jnp.concatenate([first, second], axis=1)


def gather_steps(mine):
    tokens = yield
    came = turned(after(mine, *tokens), UP, 1)
    low = jnp.concatenate([mine, came], axis=0)
    tokens = yield came
    high = turned(after(low, *tokens), UP, 0)
    yield high
    yield [low, high]


def begun(chain):
    next(chain)
    return chain


def local(gradient):
    row, col = lax.axis_index("row"), lax.axis_index("col")
    core, x, z_low = row % 2, row // 2 % 4, row // 8
    ring, y, upper = x // 2 * 2 + z_low, col // 4, x % 2
    rights = [ring, ring ^ (1 + core), ring ^ (2 - core), ring ^ 3]
    lefts = [y, y ^ (3 - 2 * core), y ^ (1 + 2 * core), y ^ 2]
    place = jnp.stack([core] + rights + lefts + [upper]).astype(jnp.int32)
    other = hop(gradient, "row", CORE)
    near = hop(lax.dynamic_slice(gradient, (0, (1 - upper) * HALF), (ROWS, HALF)), "row", NEAR)
    rights = begun(right_steps(*right_gram(place, gradient, other)))
    keep, send, grad = own_gram(place, gradient, other)
    owns = begun(scatter_steps(keep, send))
    r1, o1 = rights.send([]), owns.send([])
    near = after(near, send)
    crosses = begun(scatter_steps(*cross_gram(place, gradient, other, near)))
    c1 = crosses.send([o1])
    o2 = owns.send([])
    r2 = rights.send([])
    c2 = crosses.send([o2])
    r3 = rights.send([])
    own, cross = next(owns), next(crosses)
    deep = begun(deep_steps(jnp.concatenate([own, cross], axis=1)))
    c3 = deep.send([r2])
    r4 = rights.send([c3])
    next(deep)
    c4 = deep.send([r3])
    both = next(deep)
    r5 = rights.send([c4])
    c5, cross = pair_step(both[:, 2 * ROWS :], [r4])
    gather = begun(gather_steps(jnp.concatenate([both[:, : 2 * ROWS], cross], axis=1)))
    c6 = gather.send([r5])
    r6 = rights.send([])
    c7 = gather.send([r6])
    parts, sides = next(rights), next(gather)
    late = lax.dynamic_slice(after(gradient, r3), (0, upper * HALF), (ROWS, HALF))
    near_late = hop(late, "row", NEAR)
    far = hop(near, "row", CORE)
    far_late = hop(near_late, "row", CORE)
    rows, square = left_rows(place, sides)
    totals = spread(square)
    root = right_root(place, parts)
    tiles = [
        product(root, gradient),
        product(root, other),
        product(root, place, near, near_late),
        product(root, place, far, far_late),
    ]
    value, square = precond(totals, rows, tiles, grad)
    return graft(spread(square), value)


def solution(mesh):
    return jax.shard_map(
        local, mesh=mesh, in_specs=(P("row", "col"),), out_specs=P("row", "col"), check_vma=False
    )
```

```python
import jax
import jax.numpy as jnp
from jax import lax
from jax.experimental import pallas as pl
from jax.experimental.pallas import tpu as pltpu
from jax.sharding import PartitionSpec as P

BLOCK = 1536
ROWS = 384
LANE = 128
BLOCKS = BLOCK // LANE
BAND = 7
HALF = BLOCK // 2
RIGHT = 192
LEFT = 96
GRAFT = 96

damping = 0.001
F32 = jnp.float32
BF16 = jnp.bfloat16
MIB = 1 << 20

SMEM = pl.BlockSpec(memory_space=pltpu.SMEM)
VMEM = pl.BlockSpec(memory_space=pltpu.VMEM)
ANY = pl.BlockSpec(memory_space=pl.ANY)


def params(mib):
    return pltpu.CompilerParams(vmem_limit_bytes=mib * MIB)


def cost(flops, moved):
    return pl.CostEstimate(flops=flops, bytes_accessed=moved, transcendentals=0)


def sds(shape, dtype):
    return jax.ShapeDtypeStruct(shape, dtype)


def hop(value, axis, mask):
    return lax.ppermute(value, axis, [(i, i ^ mask) for i in range(16)])


def folded(wide):
    rows, cols = wide.shape
    tall = jnp.sum(wide.reshape(rows // 8, 8, cols), axis=0)
    total = tall[:, :LANE]
    for start in range(LANE, cols, LANE):
        total = total + tall[:, start : start + LANE]
    return total


def squares(ref):
    total = jnp.zeros((8, LANE), F32)
    for start in range(0, ref.shape[0], 48):
        part = ref[start : start + 48, :].astype(F32)
        total = total + folded(part * part)
    return total


def nt(a, b):
    return lax.dot_general(a, b, (((1,), (1,)), ((), ())), preferred_element_type=F32)


def dealt(whole, outs, rows, place, first):
    for slot in range(4):
        start = pl.multiple_of(place[first + slot] * rows, 16)
        at = slot % 2 * rows
        outs[slot // 2][at : at + rows, :] = whole[pl.ds(start, rows), :]


def right_kernel(place, mine, other, keep, send, wide, whole, sems):
    copies = []
    for at, source in enumerate((mine, other)):
        rows = pl.ds(at * ROWS, ROWS)
        copies.append(pltpu.make_async_copy(source, wide.at[rows, pl.ds(0, BLOCK)], sems.at[2 * at]))
        copies.append(
            pltpu.make_async_copy(
                source.at[:, pl.ds(0, HALF)], wide.at[rows, pl.ds(BLOCK, HALF)], sems.at[2 * at + 1]
            )
        )
    for copy in copies:
        copy.start()
    for copy in copies:
        copy.wait()
    for pair in range(3):
        start = pl.multiple_of(place[0] * HALF + pair * 256, LANE)
        strip = wide[:, pl.ds(start, 1024)]
        gram = lax.dot_general(
            strip[:, :256], strip, (((0,), (0,)), ((), ())), preferred_element_type=F32
        ).astype(BF16)
        for half in range(2):
            at = pair * 256 + half * LANE
            whole[at : at + LANE, :] = gram[
                half * LANE : half * LANE + LANE, half * LANE : half * LANE + BAND * LANE
            ]
    dealt(whole, (keep, send), RIGHT, place, 1)


def right_gram(place, mine, other):
    return pl.pallas_call(
        right_kernel,
        out_shape=[sds((2 * RIGHT, BAND * LANE), BF16)] * 2,
        in_specs=[SMEM, ANY, ANY],
        out_specs=[VMEM] * 2,
        scratch_shapes=[
            pltpu.VMEM((2 * ROWS, BLOCK + HALF), BF16),
            pltpu.VMEM((HALF, BAND * LANE), BF16),
            pltpu.SemaphoreType.DMA((4,)),
        ],
        compiler_params=params(32),
        cost_estimate=cost(10**6, 10**4),
        name="right_gram",
    )(place, mine, other)


def own_kernel(place, mine, other, keep, send, square_out, whole):
    for at, source in enumerate((mine, other)):
        whole[:, at * ROWS : (at + 1) * ROWS] = nt(mine[...], source[...]).astype(BF16)
    dealt(whole, (keep, send), LEFT, place, 5)
    square_out[...] = squares(mine)


def own_gram(place, mine, other):
    half = sds((2 * LEFT, 2 * ROWS), BF16)
    return pl.pallas_call(
        own_kernel,
        out_shape=[half, half, sds((8, LANE), F32)],
        in_specs=[SMEM, VMEM, VMEM],
        out_specs=[VMEM] * 3,
        scratch_shapes=[pltpu.VMEM((ROWS, 2 * ROWS), BF16)],
        compiler_params=params(24),
        cost_estimate=cost(10**6, 10**4),
        name="own_gram",
    )(place, mine, other)


def cross_kernel(place, mine, other, near, keep, send, whole):
    upper = place[9]
    half = pl.ds(pl.multiple_of(upper * HALF, LANE), HALF)
    for at, source in enumerate((mine, other)):
        span = slice(at * ROWS, (at + 1) * ROWS)

        @pl.when(upper == 0)
        def _():
            whole[:, span] = nt(source[:, half], near[...]).astype(BF16)

        @pl.when(upper == 1)
        def _():
            whole[:, span] = nt(near[...], source[:, half]).astype(BF16)

    dealt(whole, (keep, send), LEFT, place, 5)


def cross_gram(place, mine, other, near):
    return pl.pallas_call(
        cross_kernel,
        out_shape=[sds((2 * LEFT, 2 * ROWS), BF16)] * 2,
        in_specs=[SMEM] + [VMEM] * 3,
        out_specs=[VMEM] * 2,
        scratch_shapes=[pltpu.VMEM((ROWS, 2 * ROWS), BF16)],
        compiler_params=params(24),
        cost_estimate=cost(10**6, 10**4),
        name="cross_gram",
    )(place, mine, other, near)


def left_rows_kernel(place, low, high, rows_out, square_out, cross):
    for slot in range(4):
        rows = pl.ds(pl.multiple_of(place[5 + slot] * LEFT, 16), LEFT)
        span = slice(slot % 2 * LEFT, slot % 2 * LEFT + LEFT)
        rows_out[rows, : 2 * ROWS] = (low, high)[slot // 2][span, : 2 * ROWS]
        cross[rows, :] = (low, high)[slot // 2][span, 2 * ROWS :]

    @pl.when(place[9] == 0)
    def _():
        rows_out[:, 2 * ROWS :] = cross[...]

    @pl.when(place[9] == 1)
    def _():
        for at in range(2):
            part = cross[:, at * ROWS : (at + 1) * ROWS].astype(F32).T
            rows_out[:, (2 + at) * ROWS : (3 + at) * ROWS] = part.astype(BF16)

    own = rows_out[:, :ROWS].astype(F32)
    shape = (ROWS, ROWS)
    eye = lax.broadcasted_iota(jnp.int32, shape, 0) == lax.broadcasted_iota(jnp.int32, shape, 1)
    own = own + jnp.where(eye, damping, 0.0)
    square_out[...] = folded(own * own) + squares(rows_out.at[:, pl.ds(ROWS, BLOCK - ROWS)])


def left_rows(place, parts):
    return pl.pallas_call(
        left_rows_kernel,
        out_shape=[sds((ROWS, BLOCK), BF16), sds((8, LANE), F32)],
        in_specs=[SMEM] + [VMEM] * 2,
        out_specs=[VMEM] * 2,
        scratch_shapes=[pltpu.VMEM((ROWS, 2 * ROWS), BF16)],
        compiler_params=params(24),
        cost_estimate=cost(10**6, 2 * 10**6),
        name="left_rows",
    )(place, *parts)


def scale_of(total):
    total = jnp.sum(total, axis=1, keepdims=True)
    total = jnp.sum(total, axis=0, keepdims=True)
    return jnp.sqrt(jnp.broadcast_to(total, (1, LANE)))


def widened(row, width):
    return jnp.concatenate([row] * (width // LANE), axis=1)


def root_kernel(place, *refs):
    parts, (root, packed, sems) = refs[:4], refs[4:]
    core = place[0]
    copies = []
    for side in range(2):
        for slot in range(4):
            turned = slot if side == 0 or slot in (0, 3) else 3 - slot
            start = pl.multiple_of((core ^ side) * HALF + place[1 + turned] * RIGHT, 16)
            copies.append(
                pltpu.make_async_copy(
                    parts[2 * side + slot // 2].at[pl.ds(slot % 2 * RIGHT, RIGHT), :],
                    packed.at[pl.ds(start, RIGHT), :],
                    sems.at[4 * side + slot],
                )
            )
    for copy in copies:
        copy.start()
    for copy in copies:
        copy.wait()
    shape = (LANE, LANE)
    eye = lax.broadcasted_iota(jnp.int32, shape, 0) == lax.broadcasted_iota(jnp.int32, shape, 1)
    total = jnp.zeros((8, LANE), F32)
    for row in range(BLOCKS):
        strip = packed[row * LANE : (row + 1) * LANE, :].astype(F32)
        head = strip[:, :LANE] + jnp.where(eye, damping, 0.0)
        tail = strip[:, 6 * LANE :]
        middle = strip[:, LANE : 6 * LANE]
        total = total + folded(head * head) + folded(tail * tail) + 2.0 * folded(middle * middle)
    scale = scale_of(total)
    factor = 0.25 / jnp.sqrt(jnp.sqrt(scale))
    inverse = 1.0 / scale
    for row in range(BLOCKS):
        for apart in range(BAND):
            part = packed[row * LANE : (row + 1) * LANE, apart * LANE : (apart + 1) * LANE]
            part = part.astype(F32)
            if apart == 0:
                part = jnp.where(eye, 5.0 - (part + damping) * inverse, -part * inverse)
                part = part * factor
            else:
                part = (-part * inverse) * factor
            col = (row + apart) % BLOCKS
            root[row * LANE : (row + 1) * LANE, col * LANE : (col + 1) * LANE] = part.astype(BF16)
            if 0 < apart < 6:
                root[col * LANE : (col + 1) * LANE, row * LANE : (row + 1) * LANE] = part.T.astype(BF16)


def right_root(place, parts):
    return pl.pallas_call(
        root_kernel,
        out_shape=sds((BLOCK, BLOCK), BF16),
        in_specs=[SMEM] + [ANY] * 4,
        out_specs=VMEM,
        scratch_shapes=[pltpu.VMEM((BLOCK, BAND * LANE), BF16), pltpu.SemaphoreType.DMA((8,))],
        compiler_params=params(24),
        cost_estimate=cost(18 * 10**9, 8 * 10**6),
        name="right_root",
    )(place, *parts)


def multiply(tile, root, out):
    for start in range(0, BLOCK, 512):
        out[:, start : start + 512] = jnp.dot(
            tile[...], root[:, start : start + 512], preferred_element_type=F32
        ).astype(BF16)


def chip_product_kernel(mine, other, root, out):
    multiply(mine, root, out.at[pl.ds(0, ROWS), :])
    multiply(other, root, out.at[pl.ds(ROWS, ROWS), :])


def near_product_kernel(place, near, near_late, far, far_late, root, out, tile):
    upper = place[9]
    early = pl.ds(pl.multiple_of(upper * HALF, LANE), HALF)
    late = pl.ds(pl.multiple_of((1 - upper) * HALF, LANE), HALF)
    for at, (first, second) in enumerate(((near, near_late), (far, far_late))):
        tile[at, :, early] = first[...]
        tile[at, :, late] = second[...]
        multiply(tile.at[at], root, out.at[pl.ds(at * ROWS, ROWS), :])


def product(kernel, scratch, *refs):
    return pl.pallas_call(
        kernel,
        out_shape=sds((2 * ROWS, BLOCK), BF16),
        in_specs=[SMEM if ref.ndim == 1 else VMEM for ref in refs],
        out_specs=VMEM,
        scratch_shapes=scratch,
        compiler_params=params(24),
        cost_estimate=cost(18 * 10**9, 9 * 10**6),
        name="product",
    )(*refs)


def precond_kernel(a, b, c, d, rows, chip, near, grad, out, square_out, root):
    scale = scale_of((a[...] + b[...]) + (c[...] + d[...]))
    factor = 0.25 / jnp.sqrt(jnp.sqrt(scale))
    inverse = 1.0 / scale
    shape = (ROWS, ROWS)
    eye = lax.broadcasted_iota(jnp.int32, shape, 0) == lax.broadcasted_iota(jnp.int32, shape, 1)
    inverse, factor = widened(inverse, ROWS), widened(factor, ROWS)
    own = rows[:, :ROWS].astype(F32)
    own = jnp.where(eye, 5.0 - (own + damping) * inverse, -own * inverse) * factor
    root[:, :ROWS] = own.astype(BF16)
    for start in range(ROWS, BLOCK, ROWS):
        part = rows[:, start : start + ROWS].astype(F32)
        root[:, start : start + ROWS] = ((-part * inverse) * factor).astype(BF16)
    total = jnp.zeros((8, LANE), F32)
    for start in range(0, BLOCK, 256):
        span = slice(start, start + 256)
        part = jnp.dot(root[:, :HALF], chip[:, span], preferred_element_type=F32)
        part = part + jnp.dot(root[:, HALF:], near[:, span], preferred_element_type=F32)
        out[:, start : start + 256] = part
        total = total + folded(part * part)
    square_out[:8, :] = total
    square_out[8:, :] = grad[...]


def precond(totals, rows, tiles, grad):
    return pl.pallas_call(
        precond_kernel,
        out_shape=[sds((ROWS, BLOCK), F32), sds((16, LANE), F32)],
        in_specs=[VMEM] * 8,
        out_specs=[VMEM] * 2,
        scratch_shapes=[pltpu.VMEM((ROWS, BLOCK), BF16)],
        compiler_params=params(40),
        cost_estimate=cost(18 * 10**8, 8 * 10**6),
        name="precond",
    )(*totals, rows, *tiles, grad)


def graft_kernel(a, b, c, d, value, out, held, sems):
    total = (a[...] + b[...]) + (c[...] + d[...])
    pre = jnp.sum(jnp.sum(total[:8, :], axis=1, keepdims=True), axis=0, keepdims=True)
    factor = scale_of(total[8:, :]) / jnp.sqrt(jnp.broadcast_to(pre, (1, LANE)) + 1e-06)
    factor = widened(factor, BLOCK)
    copies = []
    for at in range(ROWS // GRAFT):
        rows = pl.ds(at * GRAFT, GRAFT)
        held[rows, :] = (value[rows, :] * factor).astype(BF16)
        copies.append(pltpu.make_async_copy(held.at[rows, :], out.at[rows, :], sems.at[at]))
        copies[-1].start()
    for copy in copies:
        copy.wait()


def graft(totals, value):
    return pl.pallas_call(
        graft_kernel,
        out_shape=sds((ROWS, BLOCK), BF16),
        in_specs=[VMEM] * 5,
        out_specs=ANY,
        scratch_shapes=[pltpu.VMEM((ROWS, BLOCK), BF16), pltpu.SemaphoreType.DMA((ROWS // GRAFT,))],
        compiler_params=params(24),
        cost_estimate=cost(10**6, 4 * 10**6),
        name="graft",
    )(*totals, value)


def total_of(a, b):
    return a.astype(F32) + b.astype(F32)


CORE, NEAR, FAR, ACROSS = 1, 2, 6, 8
ROUND = ((FAR, ACROSS), (ACROSS, FAR))
UP = ((4, 12), (12, 4))
DEEP = ((1, 3), (3, 1))


def turned(value, masks, at):
    pairs = []
    for device in range(256):
        mask = masks[device // 16 % 2][at]
        mask = mask * 16 if masks is ROUND else mask
        pairs.append((device, device ^ mask))
    return lax.ppermute(value, ("row", "col"), pairs)


def after(value, *tokens):
    return lax.optimization_barrier((value, tokens))[0]


def spread(value):
    return [value] + [hop(value, "row", mask) for mask in (CORE, NEAR, CORE | NEAR)]


def right_steps(keep, send):
    tokens = yield
    came = turned(after(send, *tokens), ROUND, 0)
    total = total_of(keep, came)
    tokens = yield came
    came = turned(after(total[RIGHT:].astype(BF16), *tokens), ROUND, 1)
    mine = total_of(total[:RIGHT], came).astype(BF16)
    tokens = yield came
    came = hop(after(mine, *tokens), "row", NEAR)
    mine = total_of(mine, came).astype(BF16)
    tokens = yield came
    came = turned(after(mine, *tokens), ROUND, 1)
    low = jnp.concatenate([mine, came], axis=0)
    tokens = yield came
    low = after(low, *tokens)
    high = turned(low, ROUND, 0)
    low_other = hop(low, "row", CORE)
    tokens = yield high
    high_other = hop(after(high, *tokens), "row", CORE)
    yield high_other
    yield [low, high, low_other, high_other]


def scatter_steps(keep, send):
    tokens = yield
    came = turned(after(send, *tokens), UP, 0)
    total = total_of(keep, came)
    tokens = yield came
    came = turned(after(total[LEFT:].astype(BF16), *tokens), UP, 1)
    yield came
    yield total_of(total[:LEFT], came).astype(BF16)


def deep_steps(mine):
    for at in range(2):
        tokens = yield
        came = turned(after(mine, *tokens), DEEP, at)
        mine = total_of(mine, came).astype(BF16)
        yield came
    yield mine


def pair_step(mine, tokens):
    mine = after(mine, *tokens)
    near = hop(mine, "row", NEAR)
    core = hop(mine[:, ROWS:], "row", CORE)
    first = total_of(mine[:, :ROWS], near[:, :ROWS]).astype(BF16)
    second = total_of(core, near[:, ROWS:]).astype(BF16)
    return near, jnp.concatenate([first, second], axis=1)


def gather_steps(mine):
    tokens = yield
    came = turned(after(mine, *tokens), UP, 1)
    low = jnp.concatenate([mine, came], axis=0)
    tokens = yield came
    high = turned(after(low, *tokens), UP, 0)
    yield high
    yield [low, high]


def begun(chain):
    next(chain)
    return chain


def local(gradient):
    row, col = lax.axis_index("row"), lax.axis_index("col")
    core, x, z_low = row % 2, row // 2 % 4, row // 8
    ring, y, upper = x // 2 * 2 + z_low, col // 4, x % 2
    rights = [ring, ring ^ (1 + core), ring ^ (2 - core), ring ^ 3]
    lefts = [y, y ^ (3 - 2 * core), y ^ (1 + 2 * core), y ^ 2]
    place = jnp.stack([core] + rights + lefts + [upper]).astype(jnp.int32)
    other = hop(gradient, "row", CORE)
    near = hop(lax.dynamic_slice(gradient, (0, (1 - upper) * HALF), (ROWS, HALF)), "row", NEAR)
    rights = begun(right_steps(*right_gram(place, gradient, other)))
    keep, send, grad = own_gram(place, gradient, other)
    owns = begun(scatter_steps(keep, send))
    r1, o1 = rights.send([]), owns.send([])
    near = after(near, send)
    crosses = begun(scatter_steps(*cross_gram(place, gradient, other, near)))
    c1 = crosses.send([o1])
    o2 = owns.send([])
    r2 = rights.send([])
    c2 = crosses.send([o2])
    r3 = rights.send([])
    own, cross = next(owns), next(crosses)
    deep = begun(deep_steps(jnp.concatenate([own, cross], axis=1)))
    c3 = deep.send([r2])
    r4 = rights.send([])
    next(deep)
    c4 = deep.send([r3])
    both = next(deep)
    r5 = rights.send([])
    late = lax.dynamic_slice(after(gradient, r3), (0, upper * HALF), (ROWS, HALF))
    near_late = hop(late, "row", NEAR)
    c5, cross = pair_step(both[:, 2 * ROWS :], [r4, near_late])
    gather = begun(gather_steps(jnp.concatenate([both[:, : 2 * ROWS], cross], axis=1)))
    c6 = gather.send([r5])
    r6 = rights.send([])
    parts = next(rights)
    root = right_root(place, parts)
    c7 = gather.send([r6])
    sides = next(gather)
    far = hop(near, "row", CORE)
    far_late = hop(near_late, "row", CORE)
    rows, square = left_rows(place, sides)
    totals = spread(square)
    scratch = [pltpu.VMEM((2, ROWS, BLOCK), BF16)]
    tiles = [
        product(chip_product_kernel, [], gradient, other, root),
        product(near_product_kernel, scratch, place, near, near_late, far, far_late, root),
    ]
    value, square = precond(totals, rows, tiles, grad)
    return graft(spread(square), value)


def solution(mesh):
    return jax.shard_map(
        local, mesh=mesh, in_specs=(P("row", "col"),), out_specs=P("row", "col"), check_vma=False
    )
```

```python
import jax
import jax.numpy as jnp
from jax import lax
from jax.experimental import pallas as pl
from jax.experimental.pallas import tpu as pltpu
from jax.sharding import PartitionSpec as P

BLOCK = 1536
ROWS = 384
LANE = 128
BLOCKS = BLOCK // LANE
BAND = 7
HALF = BLOCK // 2
RIGHT = 192
LEFT = 96
GRAFT = 96

damping = 0.001
F32 = jnp.float32
BF16 = jnp.bfloat16
MIB = 1 << 20

SMEM = pl.BlockSpec(memory_space=pltpu.SMEM)
VMEM = pl.BlockSpec(memory_space=pltpu.VMEM)
ANY = pl.BlockSpec(memory_space=pl.ANY)


def params(mib):
    return pltpu.CompilerParams(vmem_limit_bytes=mib * MIB)


def cost(flops, moved):
    return pl.CostEstimate(flops=flops, bytes_accessed=moved, transcendentals=0)


def sds(shape, dtype):
    return jax.ShapeDtypeStruct(shape, dtype)


def hop(value, axis, mask):
    return lax.ppermute(value, axis, [(i, i ^ mask) for i in range(16)])


def folded(wide):
    rows, cols = wide.shape
    tall = jnp.sum(wide.reshape(rows // 8, 8, cols), axis=0)
    total = tall[:, :LANE]
    for start in range(LANE, cols, LANE):
        total = total + tall[:, start : start + LANE]
    return total


def squares(ref):
    total = jnp.zeros((8, LANE), F32)
    for start in range(0, ref.shape[0], 48):
        part = ref[start : start + 48, :].astype(F32)
        total = total + folded(part * part)
    return total


def nt(a, b):
    return lax.dot_general(a, b, (((1,), (1,)), ((), ())), preferred_element_type=F32)


def dealt(whole, outs, rows, place, first):
    for slot in range(4):
        start = pl.multiple_of(place[first + slot] * rows, 16)
        at = slot % 2 * rows
        outs[slot // 2][at : at + rows, :] = whole[pl.ds(start, rows), :]


def right_kernel(place, mine, other, keep, send, wide, whole, sems):
    copies = []
    for at, source in enumerate((mine, other)):
        rows = pl.ds(at * ROWS, ROWS)
        copies.append(pltpu.make_async_copy(source, wide.at[rows, pl.ds(0, BLOCK)], sems.at[2 * at]))
        copies.append(
            pltpu.make_async_copy(
                source.at[:, pl.ds(0, HALF)], wide.at[rows, pl.ds(BLOCK, HALF)], sems.at[2 * at + 1]
            )
        )
    for copy in copies:
        copy.start()
    for copy in copies:
        copy.wait()
    for pair in range(3):
        start = pl.multiple_of(place[0] * HALF + pair * 256, LANE)
        strip = wide[:, pl.ds(start, 1024)]
        gram = lax.dot_general(
            strip[:, :256], strip, (((0,), (0,)), ((), ())), preferred_element_type=F32
        ).astype(BF16)
        for half in range(2):
            at = pair * 256 + half * LANE
            whole[at : at + LANE, :] = gram[
                half * LANE : half * LANE + LANE, half * LANE : half * LANE + BAND * LANE
            ]
    dealt(whole, (keep, send), RIGHT, place, 1)


def right_gram(place, mine, other):
    return pl.pallas_call(
        right_kernel,
        out_shape=[sds((2 * RIGHT, BAND * LANE), BF16)] * 2,
        in_specs=[SMEM, ANY, ANY],
        out_specs=[VMEM] * 2,
        scratch_shapes=[
            pltpu.VMEM((2 * ROWS, BLOCK + HALF), BF16),
            pltpu.VMEM((HALF, BAND * LANE), BF16),
            pltpu.SemaphoreType.DMA((4,)),
        ],
        compiler_params=params(16),
        cost_estimate=cost(10**6, 10**4),
        name="right_gram",
    )(place, mine, other)


def own_kernel(place, mine, other, keep, send, square_out, whole):
    for at, source in enumerate((mine, other)):
        whole[:, at * ROWS : (at + 1) * ROWS] = nt(mine[...], source[...]).astype(BF16)
    dealt(whole, (keep, send), LEFT, place, 5)
    square_out[...] = squares(mine)


def own_gram(place, mine, other):
    half = sds((2 * LEFT, 2 * ROWS), BF16)
    return pl.pallas_call(
        own_kernel,
        out_shape=[half, half, sds((8, LANE), F32)],
        in_specs=[SMEM, VMEM, VMEM],
        out_specs=[VMEM] * 3,
        scratch_shapes=[pltpu.VMEM((ROWS, 2 * ROWS), BF16)],
        compiler_params=params(16),
        cost_estimate=cost(10**6, 10**4),
        name="own_gram",
    )(place, mine, other)


def cross_kernel(place, mine, other, near, keep, send, whole):
    upper = place[9]
    half = pl.ds(pl.multiple_of(upper * HALF, LANE), HALF)
    for at, source in enumerate((mine, other)):
        span = slice(at * ROWS, (at + 1) * ROWS)

        @pl.when(upper == 0)
        def _():
            whole[:, span] = nt(source[:, half], near[...]).astype(BF16)

        @pl.when(upper == 1)
        def _():
            whole[:, span] = nt(near[...], source[:, half]).astype(BF16)

    dealt(whole, (keep, send), LEFT, place, 5)


def cross_gram(place, mine, other, near):
    return pl.pallas_call(
        cross_kernel,
        out_shape=[sds((2 * LEFT, 2 * ROWS), BF16)] * 2,
        in_specs=[SMEM] + [VMEM] * 3,
        out_specs=[VMEM] * 2,
        scratch_shapes=[pltpu.VMEM((ROWS, 2 * ROWS), BF16)],
        compiler_params=params(16),
        cost_estimate=cost(10**6, 10**4),
        name="cross_gram",
    )(place, mine, other, near)


def left_rows_kernel(place, low, high, rows_out, square_out, cross):
    for slot in range(4):
        rows = pl.ds(pl.multiple_of(place[5 + slot] * LEFT, 16), LEFT)
        span = slice(slot % 2 * LEFT, slot % 2 * LEFT + LEFT)
        rows_out[rows, : 2 * ROWS] = (low, high)[slot // 2][span, : 2 * ROWS]
        cross[rows, :] = (low, high)[slot // 2][span, 2 * ROWS :]

    @pl.when(place[9] == 0)
    def _():
        rows_out[:, 2 * ROWS :] = cross[...]

    @pl.when(place[9] == 1)
    def _():
        for at in range(2):
            part = cross[:, at * ROWS : (at + 1) * ROWS].astype(F32).T
            rows_out[:, (2 + at) * ROWS : (3 + at) * ROWS] = part.astype(BF16)

    own = rows_out[:, :ROWS].astype(F32)
    shape = (ROWS, ROWS)
    eye = lax.broadcasted_iota(jnp.int32, shape, 0) == lax.broadcasted_iota(jnp.int32, shape, 1)
    own = own + jnp.where(eye, damping, 0.0)
    square_out[...] = folded(own * own) + squares(rows_out.at[:, pl.ds(ROWS, BLOCK - ROWS)])


def left_rows(place, parts):
    return pl.pallas_call(
        left_rows_kernel,
        out_shape=[sds((ROWS, BLOCK), BF16), sds((8, LANE), F32)],
        in_specs=[SMEM] + [VMEM] * 2,
        out_specs=[VMEM] * 2,
        scratch_shapes=[pltpu.VMEM((ROWS, 2 * ROWS), BF16)],
        compiler_params=params(16),
        cost_estimate=cost(10**6, 2 * 10**6),
        name="left_rows",
    )(place, *parts)


def scale_of(total):
    total = jnp.sum(total, axis=1, keepdims=True)
    total = jnp.sum(total, axis=0, keepdims=True)
    return jnp.sqrt(jnp.broadcast_to(total, (1, LANE)))


def widened(row, width):
    return jnp.concatenate([row] * (width // LANE), axis=1)


def root_kernel(place, *refs):
    parts, (root, packed, sems) = refs[:4], refs[4:]
    core = place[0]
    copies, shards = [], []
    for side in range(2):
        for slot in range(4):
            turned = slot if side == 0 or slot in (0, 3) else 3 - slot
            shard = place[1 + turned]
            source = parts[2 * side + slot // 2].at[pl.ds(slot % 2 * RIGHT, RIGHT), :]
            start = pl.multiple_of((core ^ side) * HALF + shard * RIGHT, 16)
            copies.append(
                pltpu.make_async_copy(
                    source, packed.at[pl.ds(start, RIGHT), :], sems.at[4 * side + slot]
                )
            )
            shards.append((source, shard % 2 * (LANE // 2)))
    for copy in copies:
        copy.start()
    row = lax.broadcasted_iota(jnp.int32, (RIGHT, LANE), 0)
    lane = lax.broadcasted_iota(jnp.int32, (RIGHT, LANE), 1)
    total = jnp.zeros((8, LANE), F32)
    for source, shift in shards:
        diagonal = lax.rem(row + shift, LANE) == lane
        head = source[:, :LANE].astype(F32) + jnp.where(diagonal, damping, 0.0)
        tail = source[:, 6 * LANE :].astype(F32)
        middle = source[:, LANE : 6 * LANE].astype(F32)
        total = total + folded(head * head + tail * tail) + 2.0 * folded(middle * middle)
    scale = scale_of(total)
    factor = 0.25 / jnp.sqrt(jnp.sqrt(scale))
    inverse = 1.0 / scale
    shape = (LANE, LANE)
    eye = lax.broadcasted_iota(jnp.int32, shape, 0) == lax.broadcasted_iota(jnp.int32, shape, 1)
    for copy in copies:
        copy.wait()
    for row in range(BLOCKS):
        for apart in range(BAND):
            part = packed[row * LANE : (row + 1) * LANE, apart * LANE : (apart + 1) * LANE]
            part = part.astype(F32)
            if apart == 0:
                part = jnp.where(eye, 5.0 - (part + damping) * inverse, -part * inverse)
                part = part * factor
            else:
                part = (-part * inverse) * factor
            part = part.astype(BF16)
            col = (row + apart) % BLOCKS
            root[row * LANE : (row + 1) * LANE, col * LANE : (col + 1) * LANE] = part
            if 0 < apart < 6:
                root[col * LANE : (col + 1) * LANE, row * LANE : (row + 1) * LANE] = part.T


def right_root(place, parts):
    return pl.pallas_call(
        root_kernel,
        out_shape=sds((BLOCK, BLOCK), BF16),
        in_specs=[SMEM] + [VMEM] * 4,
        out_specs=VMEM,
        scratch_shapes=[pltpu.VMEM((BLOCK, BAND * LANE), BF16), pltpu.SemaphoreType.DMA((8,))],
        compiler_params=params(16),
        cost_estimate=cost(18 * 10**9, 8 * 10**6),
        name="right_root",
    )(place, *parts)


def multiply(tile, root, out):
    for start in range(0, BLOCK, 512):
        out[:, start : start + 512] = jnp.dot(
            tile[...], root[:, start : start + 512], preferred_element_type=F32
        ).astype(BF16)


def chip_product_kernel(mine, other, root, out):
    multiply(mine, root, out.at[pl.ds(0, ROWS), :])
    multiply(other, root, out.at[pl.ds(ROWS, ROWS), :])


def near_product_kernel(place, near, near_late, far, far_late, root, out, tile):
    upper = place[9]
    early = pl.ds(pl.multiple_of(upper * HALF, LANE), HALF)
    late = pl.ds(pl.multiple_of((1 - upper) * HALF, LANE), HALF)
    for at, (first, second) in enumerate(((near, near_late), (far, far_late))):
        tile[at, :, early] = first[...]
        tile[at, :, late] = second[...]
        multiply(tile.at[at], root, out.at[pl.ds(at * ROWS, ROWS), :])


def product(kernel, scratch, *refs):
    return pl.pallas_call(
        kernel,
        out_shape=sds((2 * ROWS, BLOCK), BF16),
        in_specs=[SMEM if ref.ndim == 1 else VMEM for ref in refs],
        out_specs=VMEM,
        scratch_shapes=scratch,
        compiler_params=params(16),
        cost_estimate=cost(18 * 10**9, 9 * 10**6),
        name="product",
    )(*refs)


def precond_kernel(a, b, c, d, rows, chip, near, grad, out, square_out, root):
    scale = scale_of((a[...] + b[...]) + (c[...] + d[...]))
    factor = 0.25 / jnp.sqrt(jnp.sqrt(scale))
    inverse = 1.0 / scale
    shape = (ROWS, ROWS)
    eye = lax.broadcasted_iota(jnp.int32, shape, 0) == lax.broadcasted_iota(jnp.int32, shape, 1)
    inverse, factor = widened(inverse, ROWS), widened(factor, ROWS)
    own = rows[:, :ROWS].astype(F32)
    own = jnp.where(eye, 5.0 - (own + damping) * inverse, -own * inverse) * factor
    root[:, :ROWS] = own.astype(BF16)
    for start in range(ROWS, BLOCK, ROWS):
        part = rows[:, start : start + ROWS].astype(F32)
        root[:, start : start + ROWS] = ((-part * inverse) * factor).astype(BF16)
    total = jnp.zeros((8, LANE), F32)
    for start in range(0, BLOCK, 256):
        span = slice(start, start + 256)
        part = jnp.dot(root[:, :HALF], chip[:, span], preferred_element_type=F32)
        part = part + jnp.dot(root[:, HALF:], near[:, span], preferred_element_type=F32)
        out[:, start : start + 256] = part
        total = total + folded(part * part)
    square_out[:8, :] = total
    square_out[8:, :] = grad[...]


def precond(totals, rows, tiles, grad):
    return pl.pallas_call(
        precond_kernel,
        out_shape=[sds((ROWS, BLOCK), F32), sds((16, LANE), F32)],
        in_specs=[VMEM] * 8,
        out_specs=[VMEM] * 2,
        scratch_shapes=[pltpu.VMEM((ROWS, BLOCK), BF16)],
        compiler_params=params(16),
        cost_estimate=cost(18 * 10**8, 8 * 10**6),
        name="precond",
    )(*totals, rows, *tiles, grad)


def graft_kernel(a, b, c, d, value, out, held, sems):
    total = (a[...] + b[...]) + (c[...] + d[...])
    pre = jnp.sum(jnp.sum(total[:8, :], axis=1, keepdims=True), axis=0, keepdims=True)
    factor = scale_of(total[8:, :]) / jnp.sqrt(jnp.broadcast_to(pre, (1, LANE)) + 1e-06)
    factor = widened(factor, BLOCK)
    copies = []
    for at in range(ROWS // GRAFT):
        rows = pl.ds(at * GRAFT, GRAFT)
        held[rows, :] = (value[rows, :] * factor).astype(BF16)
        copies.append(pltpu.make_async_copy(held.at[rows, :], out.at[rows, :], sems.at[at]))
        copies[-1].start()
    for copy in copies:
        copy.wait()


def graft(totals, value):
    return pl.pallas_call(
        graft_kernel,
        out_shape=sds((ROWS, BLOCK), BF16),
        in_specs=[VMEM] * 5,
        out_specs=ANY,
        scratch_shapes=[pltpu.VMEM((ROWS, BLOCK), BF16), pltpu.SemaphoreType.DMA((ROWS // GRAFT,))],
        compiler_params=params(16),
        cost_estimate=cost(10**6, 4 * 10**6),
        name="graft",
    )(*totals, value)


def total_of(a, b):
    return a.astype(F32) + b.astype(F32)


CORE, NEAR, FAR, ACROSS = 1, 2, 6, 8
ROUND = ((FAR, ACROSS), (ACROSS, FAR))
BACK = ROUND
UP = ((4, 12), (12, 4))
DEEP = ((1, 3), (3, 1))


def turned(value, masks, at):
    pairs = []
    for device in range(256):
        mask = masks[device // 16 % 2][at]
        mask = mask * 16 if masks in (ROUND, BACK) else mask
        pairs.append((device, device ^ mask))
    return lax.ppermute(value, ("row", "col"), pairs)


def after(value, *tokens):
    return lax.optimization_barrier((value, tokens))[0]


def spread(value):
    return [value] + [hop(value, "row", mask) for mask in (CORE, NEAR, CORE | NEAR)]


def right_steps(keep, send):
    tokens = yield
    came = turned(after(send, *tokens), ROUND, 0)
    total = total_of(keep, came)
    tokens = yield came
    came = turned(after(total[RIGHT:].astype(BF16), *tokens), ROUND, 1)
    mine = total_of(total[:RIGHT], came).astype(BF16)
    tokens = yield came
    came = hop(after(mine, *tokens), "row", NEAR)
    mine = total_of(mine, came).astype(BF16)
    tokens = yield came
    came = turned(after(mine, *tokens), BACK, 1)
    low = jnp.concatenate([mine, came], axis=0)
    tokens = yield came
    low = after(low, *tokens)
    high = turned(low, BACK, 0)
    low_other = hop(low, "row", CORE)
    tokens = yield high
    high_other = hop(after(high, *tokens), "row", CORE)
    yield high_other
    yield [low, high, low_other, high_other]


def scatter_steps(keep, send):
    tokens = yield
    came = turned(after(send, *tokens), UP, 0)
    total = total_of(keep, came)
    tokens = yield came
    came = turned(after(total[LEFT:].astype(BF16), *tokens), UP, 1)
    yield came
    yield total_of(total[:LEFT], came).astype(BF16)


def deep_steps(mine):
    for at in range(2):
        tokens = yield
        came = turned(after(mine, *tokens), DEEP, at)
        mine = total_of(mine, came).astype(BF16)
        yield came
    yield mine


def pair_step(mine, tokens):
    mine = after(mine, *tokens)
    near = hop(mine, "row", NEAR)
    core = hop(mine[:, ROWS:], "row", CORE)
    first = total_of(mine[:, :ROWS], near[:, :ROWS]).astype(BF16)
    second = total_of(core, near[:, ROWS:]).astype(BF16)
    return [near, core], jnp.concatenate([first, second], axis=1)


def gather_steps(mine):
    tokens = yield
    mine = after(mine, *tokens)
    came = turned(mine, UP, 1)
    tokens = yield came
    low = jnp.concatenate([after(mine, *tokens), came], axis=0)
    high = turned(low, UP, 0)
    yield high
    yield [low, high]


def begun(chain):
    next(chain)
    return chain


def local(gradient):
    row, col = lax.axis_index("row"), lax.axis_index("col")
    core, x, z_low = row % 2, row // 2 % 4, row // 8
    ring, y, upper = x // 2 * 2 + z_low, col // 4, x % 2
    rights = [ring, ring ^ (1 + core), ring ^ (2 - core), ring ^ 3]
    lefts = [y, y ^ (3 - 2 * core), y ^ (1 + 2 * core), y ^ 2]
    place = jnp.stack([core] + rights + lefts + [upper]).astype(jnp.int32)
    other = hop(gradient, "row", CORE)
    near = hop(lax.dynamic_slice(gradient, (0, (1 - upper) * HALF), (ROWS, HALF)), "row", NEAR)
    rights = begun(right_steps(*right_gram(place, gradient, other)))
    keep, send, grad = own_gram(place, gradient, other)
    owns = begun(scatter_steps(keep, send))
    r1, o1 = rights.send([]), owns.send([])
    near = after(near, send)
    crosses = begun(scatter_steps(*cross_gram(place, gradient, other, near)))
    c1 = crosses.send([o1])
    o2 = owns.send([])
    r2 = rights.send([])
    c2 = crosses.send([o2, r1])
    r3 = rights.send([])
    own, cross = next(owns), next(crosses)
    deep = begun(deep_steps(jnp.concatenate([own, cross], axis=1)))
    c3 = deep.send([r2])
    r4 = rights.send([])
    next(deep)
    c4 = deep.send([r3])
    both = next(deep)
    r5 = rights.send([])
    late = lax.dynamic_slice(after(gradient, r3), (0, upper * HALF), (ROWS, HALF))
    near_late = hop(late, "row", NEAR)
    c5, cross = pair_step(both[:, 2 * ROWS :], [r4, near_late])
    gather = begun(gather_steps(jnp.concatenate([both[:, : 2 * ROWS], cross], axis=1)))
    c6 = gather.send([r5])
    r6 = rights.send(c5)
    parts = next(rights)
    root = right_root(place, parts)
    c7 = gather.send([root])
    far = hop(after(near, root), "row", CORE)
    far_late = hop(after(near_late, root), "row", CORE)
    sides = next(gather)
    scratch = [pltpu.VMEM((2, ROWS, BLOCK), BF16)]
    tiles = [
        product(chip_product_kernel, [], gradient, other, root),
        product(near_product_kernel, scratch, place, near, near_late, far, far_late, root),
    ]
    rows, square = left_rows(place, after(sides, *tiles))
    totals = spread(square)
    value, square = precond(totals, rows, tiles, grad)
    return graft(spread(square), value)


def solution(mesh):
    return jax.shard_map(
        local, mesh=mesh, in_specs=(P("row", "col"),), out_specs=P("row", "col"), check_vma=False
    )
```

```python
import jax
import jax.numpy as jnp
from jax import lax
from jax.experimental import pallas as pl
from jax.experimental.pallas import tpu as pltpu
from jax.sharding import PartitionSpec as P

BLOCK = 1536
ROWS = 384
LANE = 128
BLOCKS = BLOCK // LANE
BAND = 7
HALF = BLOCK // 2
RIGHT = 192
LEFT = 96
GRAFT = 96

damping = 0.001
F32 = jnp.float32
BF16 = jnp.bfloat16
MIB = 1 << 20

SMEM = pl.BlockSpec(memory_space=pltpu.SMEM)
VMEM = pl.BlockSpec(memory_space=pltpu.VMEM)
ANY = pl.BlockSpec(memory_space=pl.ANY)


def params(mib):
    return pltpu.CompilerParams(vmem_limit_bytes=mib * MIB)


def cost(flops, moved):
    return pl.CostEstimate(flops=flops, bytes_accessed=moved, transcendentals=0)


def sds(shape, dtype):
    return jax.ShapeDtypeStruct(shape, dtype)


def hop(value, axis, mask):
    return lax.ppermute(value, axis, [(i, i ^ mask) for i in range(16)])


def folded(wide):
    rows, cols = wide.shape
    tall = jnp.sum(wide.reshape(rows // 8, 8, cols), axis=0)
    total = tall[:, :LANE]
    for start in range(LANE, cols, LANE):
        total = total + tall[:, start : start + LANE]
    return total


def squares(ref):
    total = jnp.zeros((8, LANE), F32)
    for start in range(0, ref.shape[0], 48):
        part = ref[start : start + 48, :].astype(F32)
        total = total + folded(part * part)
    return total


def nt(a, b):
    return lax.dot_general(a, b, (((1,), (1,)), ((), ())), preferred_element_type=F32)


def dealt(whole, outs, rows, place, first):
    for slot in range(4):
        start = pl.multiple_of(place[first + slot] * rows, 16)
        at = slot % 2 * rows
        outs[slot // 2][at : at + rows, :] = whole[pl.ds(start, rows), :]


def right_kernel(place, mine, other, keep, send, wide, whole, sems):
    copies = []
    for at, source in enumerate((mine, other)):
        rows = pl.ds(at * ROWS, ROWS)
        copies.append(pltpu.make_async_copy(source, wide.at[rows, pl.ds(0, BLOCK)], sems.at[2 * at]))
        copies.append(
            pltpu.make_async_copy(
                source.at[:, pl.ds(0, HALF)], wide.at[rows, pl.ds(BLOCK, HALF)], sems.at[2 * at + 1]
            )
        )
    for copy in copies:
        copy.start()
    for copy in copies:
        copy.wait()
    for pair in range(3):
        start = pl.multiple_of(place[0] * HALF + pair * 256, LANE)
        strip = wide[:, pl.ds(start, 1024)]
        gram = lax.dot_general(
            strip[:, :256], strip, (((0,), (0,)), ((), ())), preferred_element_type=F32
        ).astype(BF16)
        for half in range(2):
            at = pair * 256 + half * LANE
            whole[at : at + LANE, :] = gram[
                half * LANE : half * LANE + LANE, half * LANE : half * LANE + BAND * LANE
            ]
    dealt(whole, (keep, send), RIGHT, place, 1)


def right_gram(place, mine, other):
    return pl.pallas_call(
        right_kernel,
        out_shape=[sds((2 * RIGHT, BAND * LANE), BF16)] * 2,
        in_specs=[SMEM, ANY, ANY],
        out_specs=[VMEM] * 2,
        scratch_shapes=[
            pltpu.VMEM((2 * ROWS, BLOCK + HALF), BF16),
            pltpu.VMEM((HALF, BAND * LANE), BF16),
            pltpu.SemaphoreType.DMA((4,)),
        ],
        compiler_params=params(16),
        cost_estimate=cost(10**6, 10**4),
        name="right_gram",
    )(place, mine, other)


def own_kernel(place, mine, other, keep, send, square_out, whole):
    for at, source in enumerate((mine, other)):
        whole[:, at * ROWS : (at + 1) * ROWS] = nt(mine[...], source[...]).astype(BF16)
    dealt(whole, (keep, send), LEFT, place, 5)
    square_out[...] = squares(mine)


def own_gram(place, mine, other):
    half = sds((2 * LEFT, 2 * ROWS), BF16)
    return pl.pallas_call(
        own_kernel,
        out_shape=[half, half, sds((8, LANE), F32)],
        in_specs=[SMEM, VMEM, VMEM],
        out_specs=[VMEM] * 3,
        scratch_shapes=[pltpu.VMEM((ROWS, 2 * ROWS), BF16)],
        compiler_params=params(16),
        cost_estimate=cost(10**6, 10**4),
        name="own_gram",
    )(place, mine, other)


def cross_kernel(place, mine, other, near, keep, send, whole):
    upper = place[9]
    half = pl.ds(pl.multiple_of(upper * HALF, LANE), HALF)
    for at, source in enumerate((mine, other)):
        span = slice(at * ROWS, (at + 1) * ROWS)

        @pl.when(upper == 0)
        def _():
            whole[:, span] = nt(source[:, half], near[...]).astype(BF16)

        @pl.when(upper == 1)
        def _():
            whole[:, span] = nt(near[...], source[:, half]).astype(BF16)

    dealt(whole, (keep, send), LEFT, place, 5)


def cross_gram(place, mine, other, near):
    return pl.pallas_call(
        cross_kernel,
        out_shape=[sds((2 * LEFT, 2 * ROWS), BF16)] * 2,
        in_specs=[SMEM] + [VMEM] * 3,
        out_specs=[VMEM] * 2,
        scratch_shapes=[pltpu.VMEM((ROWS, 2 * ROWS), BF16)],
        compiler_params=params(16),
        cost_estimate=cost(10**6, 10**4),
        name="cross_gram",
    )(place, mine, other, near)


def left_rows_kernel(place, own_low, own_high, cross_low, cross_high, rows_out, square_out, cross):
    for slot in range(4):
        rows = pl.ds(pl.multiple_of(place[5 + slot] * LEFT, 16), LEFT)
        span = slice(slot % 2 * LEFT, slot % 2 * LEFT + LEFT)
        rows_out[rows, : 2 * ROWS] = (own_low, own_high)[slot // 2][span, :]
        cross[rows, :] = (cross_low, cross_high)[slot // 2][span, :]

    @pl.when(place[9] == 0)
    def _():
        rows_out[:, 2 * ROWS :] = cross[...]

    @pl.when(place[9] == 1)
    def _():
        for at in range(2):
            part = cross[:, at * ROWS : (at + 1) * ROWS].astype(F32).T
            rows_out[:, (2 + at) * ROWS : (3 + at) * ROWS] = part.astype(BF16)

    own = rows_out[:, :ROWS].astype(F32)
    shape = (ROWS, ROWS)
    eye = lax.broadcasted_iota(jnp.int32, shape, 0) == lax.broadcasted_iota(jnp.int32, shape, 1)
    own = own + jnp.where(eye, damping, 0.0)
    square_out[...] = folded(own * own) + squares(rows_out.at[:, pl.ds(ROWS, BLOCK - ROWS)])


def left_rows(place, parts):
    return pl.pallas_call(
        left_rows_kernel,
        out_shape=[sds((ROWS, BLOCK), BF16), sds((8, LANE), F32)],
        in_specs=[SMEM] + [VMEM] * 4,
        out_specs=[VMEM] * 2,
        scratch_shapes=[pltpu.VMEM((ROWS, 2 * ROWS), BF16)],
        compiler_params=params(16),
        cost_estimate=cost(10**6, 2 * 10**6),
        name="left_rows",
    )(place, *parts)


def scale_of(total):
    total = jnp.sum(total, axis=1, keepdims=True)
    total = jnp.sum(total, axis=0, keepdims=True)
    return jnp.sqrt(jnp.broadcast_to(total, (1, LANE)))


def widened(row, width):
    return jnp.concatenate([row] * (width // LANE), axis=1)


def root_kernel(place, *refs):
    parts, (root, packed, sems) = refs[:4], refs[4:]
    core = place[0]
    copies, shards = [], []
    for side in range(2):
        for slot in range(4):
            turned = slot if side == 0 or slot in (0, 3) else 3 - slot
            shard = place[1 + turned]
            source = parts[2 * side + slot // 2].at[pl.ds(slot % 2 * RIGHT, RIGHT), :]
            start = pl.multiple_of((core ^ side) * HALF + shard * RIGHT, 16)
            copies.append(
                pltpu.make_async_copy(
                    source, packed.at[pl.ds(start, RIGHT), :], sems.at[4 * side + slot]
                )
            )
            shards.append((source, shard % 2 * (LANE // 2)))
    for copy in copies:
        copy.start()
    row = lax.broadcasted_iota(jnp.int32, (RIGHT, LANE), 0)
    lane = lax.broadcasted_iota(jnp.int32, (RIGHT, LANE), 1)
    total = jnp.zeros((8, LANE), F32)
    for source, shift in shards:
        diagonal = lax.rem(row + shift, LANE) == lane
        head = source[:, :LANE].astype(F32) + jnp.where(diagonal, damping, 0.0)
        tail = source[:, 6 * LANE :].astype(F32)
        middle = source[:, LANE : 6 * LANE].astype(F32)
        total = total + folded(head * head + tail * tail) + 2.0 * folded(middle * middle)
    scale = scale_of(total)
    factor = 0.25 / jnp.sqrt(jnp.sqrt(scale))
    inverse = 1.0 / scale
    shape = (LANE, LANE)
    eye = lax.broadcasted_iota(jnp.int32, shape, 0) == lax.broadcasted_iota(jnp.int32, shape, 1)
    for copy in copies:
        copy.wait()
    for row in range(BLOCKS):
        for apart in range(BAND):
            part = packed[row * LANE : (row + 1) * LANE, apart * LANE : (apart + 1) * LANE]
            part = part.astype(F32)
            if apart == 0:
                part = jnp.where(eye, 5.0 - (part + damping) * inverse, -part * inverse)
                part = part * factor
            else:
                part = (-part * inverse) * factor
            part = part.astype(BF16)
            col = (row + apart) % BLOCKS
            root[row * LANE : (row + 1) * LANE, col * LANE : (col + 1) * LANE] = part
            if 0 < apart < 6:
                root[col * LANE : (col + 1) * LANE, row * LANE : (row + 1) * LANE] = part.T


def right_root(place, parts):
    return pl.pallas_call(
        root_kernel,
        out_shape=sds((BLOCK, BLOCK), BF16),
        in_specs=[SMEM] + [VMEM] * 4,
        out_specs=VMEM,
        scratch_shapes=[pltpu.VMEM((BLOCK, BAND * LANE), BF16), pltpu.SemaphoreType.DMA((8,))],
        compiler_params=params(16),
        cost_estimate=cost(18 * 10**9, 8 * 10**6),
        name="right_root",
    )(place, *parts)


def multiply(tile, root, out):
    for start in range(0, BLOCK, 512):
        out[:, start : start + 512] = jnp.dot(
            tile[...], root[:, start : start + 512], preferred_element_type=F32
        ).astype(BF16)


def chip_product_kernel(mine, other, root, out):
    multiply(mine, root, out.at[pl.ds(0, ROWS), :])
    multiply(other, root, out.at[pl.ds(ROWS, ROWS), :])


def near_product_kernel(place, near, near_late, far, far_late, root, out, tile):
    upper = place[9]
    early = pl.ds(pl.multiple_of(upper * HALF, LANE), HALF)
    late = pl.ds(pl.multiple_of((1 - upper) * HALF, LANE), HALF)
    for at, (first, second) in enumerate(((near, near_late), (far, far_late))):
        tile[at, :, early] = first[...]
        tile[at, :, late] = second[...]
        multiply(tile.at[at], root, out.at[pl.ds(at * ROWS, ROWS), :])


def product(kernel, scratch, *refs):
    return pl.pallas_call(
        kernel,
        out_shape=sds((2 * ROWS, BLOCK), BF16),
        in_specs=[SMEM if ref.ndim == 1 else VMEM for ref in refs],
        out_specs=VMEM,
        scratch_shapes=scratch,
        compiler_params=params(16),
        cost_estimate=cost(18 * 10**9, 9 * 10**6),
        name="product",
    )(*refs)


def precond_kernel(a, b, c, d, rows, chip, near, grad, out, square_out, root):
    scale = scale_of((a[...] + b[...]) + (c[...] + d[...]))
    factor = 0.25 / jnp.sqrt(jnp.sqrt(scale))
    inverse = 1.0 / scale
    shape = (ROWS, ROWS)
    eye = lax.broadcasted_iota(jnp.int32, shape, 0) == lax.broadcasted_iota(jnp.int32, shape, 1)
    inverse, factor = widened(inverse, ROWS), widened(factor, ROWS)
    own = rows[:, :ROWS].astype(F32)
    own = jnp.where(eye, 5.0 - (own + damping) * inverse, -own * inverse) * factor
    root[:, :ROWS] = own.astype(BF16)
    for start in range(ROWS, BLOCK, ROWS):
        part = rows[:, start : start + ROWS].astype(F32)
        root[:, start : start + ROWS] = ((-part * inverse) * factor).astype(BF16)
    total = jnp.zeros((8, LANE), F32)
    for start in range(0, BLOCK, 256):
        span = slice(start, start + 256)
        part = jnp.dot(root[:, :HALF], chip[:, span], preferred_element_type=F32)
        part = part + jnp.dot(root[:, HALF:], near[:, span], preferred_element_type=F32)
        out[:, start : start + 256] = part
        total = total + folded(part * part)
    square_out[:8, :] = total
    square_out[8:, :] = grad[...]


def precond(totals, rows, tiles, grad):
    return pl.pallas_call(
        precond_kernel,
        out_shape=[sds((ROWS, BLOCK), F32), sds((16, LANE), F32)],
        in_specs=[VMEM] * 8,
        out_specs=[VMEM] * 2,
        scratch_shapes=[pltpu.VMEM((ROWS, BLOCK), BF16)],
        compiler_params=params(16),
        cost_estimate=cost(18 * 10**8, 8 * 10**6),
        name="precond",
    )(*totals, rows, *tiles, grad)


def graft_kernel(a, b, c, d, value, out, held, sems):
    total = (a[...] + b[...]) + (c[...] + d[...])
    pre = jnp.sum(jnp.sum(total[:8, :], axis=1, keepdims=True), axis=0, keepdims=True)
    factor = scale_of(total[8:, :]) / jnp.sqrt(jnp.broadcast_to(pre, (1, LANE)) + 1e-06)
    factor = widened(factor, BLOCK)
    copies = []
    for at in range(ROWS // GRAFT):
        rows = pl.ds(at * GRAFT, GRAFT)
        held[rows, :] = (value[rows, :] * factor).astype(BF16)
        copies.append(pltpu.make_async_copy(held.at[rows, :], out.at[rows, :], sems.at[at]))
        copies[-1].start()
    for copy in copies:
        copy.wait()


def graft(totals, value):
    return pl.pallas_call(
        graft_kernel,
        out_shape=sds((ROWS, BLOCK), BF16),
        in_specs=[VMEM] * 5,
        out_specs=ANY,
        scratch_shapes=[pltpu.VMEM((ROWS, BLOCK), BF16), pltpu.SemaphoreType.DMA((ROWS // GRAFT,))],
        compiler_params=params(16),
        cost_estimate=cost(10**6, 4 * 10**6),
        name="graft",
    )(*totals, value)


def total_of(a, b):
    return a.astype(F32) + b.astype(F32)


CORE, NEAR, FAR, ACROSS = 1, 2, 6, 8
ROUND = ((FAR, ACROSS), (ACROSS, FAR))
BACK = ROUND
UP = ((4, 12), (12, 4))
DEEP = ((1, 3), (3, 1))


def turned(value, masks, at):
    pairs = []
    for device in range(256):
        mask = masks[device // 16 % 2][at]
        mask = mask * 16 if masks in (ROUND, BACK) else mask
        pairs.append((device, device ^ mask))
    return lax.ppermute(value, ("row", "col"), pairs)


def after(value, *tokens):
    return lax.optimization_barrier((value, tokens))[0]


def spread(value):
    return [value] + [hop(value, "row", mask) for mask in (CORE, NEAR, CORE | NEAR)]


def right_steps(keep, send):
    tokens = yield
    came = turned(after(send, *tokens), ROUND, 0)
    total = total_of(keep, came)
    tokens = yield came
    came = turned(after(total[RIGHT:].astype(BF16), *tokens), ROUND, 1)
    mine = total_of(total[:RIGHT], came).astype(BF16)
    tokens = yield came
    came = hop(after(mine, *tokens), "row", NEAR)
    mine = total_of(mine, came).astype(BF16)
    tokens = yield came
    came = turned(after(mine, *tokens), BACK, 1)
    low = jnp.concatenate([mine, came], axis=0)
    tokens = yield came
    low = after(low, *tokens)
    high = turned(low, BACK, 0)
    low_other = hop(low, "row", CORE)
    tokens = yield high
    high_other = hop(after(high, *tokens), "row", CORE)
    yield high_other
    yield [low, high, low_other, high_other]


def scatter_steps(keep, send):
    tokens = yield
    came = turned(after(send, *tokens), UP, 0)
    total = total_of(keep, came)
    tokens = yield came
    came = turned(after(total[LEFT:].astype(BF16), *tokens), UP, 1)
    yield came
    yield total_of(total[:LEFT], came).astype(BF16)


def deep_steps(mine):
    for at in range(2):
        tokens = yield
        came = turned(after(mine, *tokens), DEEP, at)
        mine = total_of(mine, came).astype(BF16)
        yield came
    yield mine


def pair_step(mine, tokens):
    mine = after(mine, *tokens)
    near = hop(mine, "row", NEAR)
    core = hop(mine[:, ROWS:], "row", CORE)
    first = total_of(mine[:, :ROWS], near[:, :ROWS]).astype(BF16)
    second = total_of(core, near[:, ROWS:]).astype(BF16)
    return [near, core], jnp.concatenate([first, second], axis=1)


def gather_steps(mine):
    tokens = yield
    mine = after(mine, *tokens)
    came = turned(mine, UP, 1)
    tokens = yield came
    low = jnp.concatenate([after(mine, *tokens), came], axis=0)
    high = turned(low, UP, 0)
    yield high
    yield [low, high]


def begun(chain):
    next(chain)
    return chain


def local(gradient):
    row, col = lax.axis_index("row"), lax.axis_index("col")
    core, x, z_low = row % 2, row // 2 % 4, row // 8
    ring, y, upper = x // 2 * 2 + z_low, col // 4, x % 2
    rights = [ring, ring ^ (1 + core), ring ^ (2 - core), ring ^ 3]
    lefts = [y, y ^ (3 - 2 * core), y ^ (1 + 2 * core), y ^ 2]
    place = jnp.stack([core] + rights + lefts + [upper]).astype(jnp.int32)
    other = hop(gradient, "row", CORE)
    near = hop(lax.dynamic_slice(gradient, (0, (1 - upper) * HALF), (ROWS, HALF)), "row", NEAR)
    rights = begun(right_steps(*right_gram(place, gradient, other)))
    keep, send, grad = own_gram(place, gradient, other)
    owns = begun(scatter_steps(keep, send))
    r1, o1 = rights.send([]), owns.send([])
    near = after(near, send)
    crosses = begun(scatter_steps(*cross_gram(place, gradient, other, near)))
    c1 = crosses.send([o1])
    o2 = owns.send([])
    r2 = rights.send([])
    c2 = crosses.send([o2, r1])
    r3 = rights.send([])
    own, cross = next(owns), next(crosses)
    deep = begun(deep_steps(jnp.concatenate([own, cross], axis=1)))
    c3 = deep.send([r2])
    r4 = rights.send([])
    next(deep)
    c4 = deep.send([r3])
    both = next(deep)
    r5 = rights.send([])
    late = lax.dynamic_slice(after(gradient, r3), (0, upper * HALF), (ROWS, HALF))
    near_late = hop(late, "row", NEAR)
    c5, cross = pair_step(both[:, 2 * ROWS :], [r4, near_late])
    gather = begun(gather_steps(both[:, : 2 * ROWS]))
    o5 = gather.send([])
    cross_gather = begun(gather_steps(cross))
    c6 = cross_gather.send([r5])
    o6 = gather.send([])
    r6 = rights.send([*c5, o5])
    parts = next(rights)
    root = right_root(place, parts)
    c7 = cross_gather.send([root])
    far = hop(after(near, root), "row", CORE)
    far_late = hop(after(near_late, root), "row", CORE)
    sides = next(gather) + next(cross_gather)
    scratch = [pltpu.VMEM((2, ROWS, BLOCK), BF16)]
    tiles = [
        product(chip_product_kernel, [], gradient, other, root),
        product(near_product_kernel, scratch, place, near, near_late, far, far_late, root),
    ]
    rows, square = left_rows(place, after(sides, tiles[0]))
    totals = spread(square)
    value, square = precond(totals, rows, tiles, grad)
    return graft(spread(square), value)


def solution(mesh):
    return jax.shard_map(
        local, mesh=mesh, in_specs=(P("row", "col"),), out_specs=P("row", "col"), check_vma=False
    )
```
